512 devices in a mesh: cell: 64 (over z, x_hi, core), bin: 8 (over y, x_lo).
Axes of the slice: x: 4 (x_hi: 2, x_lo: 2; x = x_hi * 2 + x_lo), y: 4, z: 16, core: 2. Of those that a mesh axis runs over, the one named last changes fastest.
Arguments:
- density: float32 [256, 512, 128], P('bin', 'cell'), may hold values from 0.01 to 1
- velocity: float32 [2, 512, 128], P(None, ('cell', 'bin')), may hold values from 0.02 to 0.35
- growth: float32 [512, 128], P('cell'), may hold values from 0.02 to 0.3
- rate: float32 [512, 128], P('cell'), may hold values from 0.1 to 1
- kernel: float32 [256], replicated, may hold values from 0.002 to 0.05
- direction: int32 [512, 128], P('cell'), may hold values from 0 to 1
- neighbour: int32 [512, 128], P('cell'), may hold values from 0 to 127
Outputs:
- final_density: float32 [256, 512, 128], P('bin', 'cell')
The draws below stay inside these ranges and needn't reach their ends.
Inputs may be any that keep to these rules, and one draw needn't show every extreme that they name: `direction`: 0 takes the row below in index, 1 the row above. `neighbour`: each entry names a cell of the same row.
All inputs are finite; a program needn't handle non-finite values.
Results may differ from the reference program's by a relative error of at most 0.0001.
Values sent between devices are 32-bit elements; how exact they have to be, the bound alone decides.
A program may use at most 64 MiB of HBM per device.

```python
import math
import jax
import jax.numpy as jnp
from jax import lax

NB = 256
CY = 128
CX = 8
STEPS = 3
NX = 512


def set_ends(values, stream_key, low, top_value):
    spot = [jax.random.randint(jax.random.fold_in(stream_key, axis), (), 0, length) for axis, length in enumerate(values.shape)]
    longest = values.shape.index(max(values.shape))
    beside = spot[:longest] + [(spot[longest] + 1) % values.shape[longest]] + spot[longest + 1:]
    return values.at[tuple(spot)].set(low).at[tuple(beside)].set(top_value)


def block_scale(rng, extent, cuts, smallest, high):
    gain, own = 1.0, jax.random.fold_in(rng, 6)
    for axis_at, parts in cuts:
        steps = jnp.exp(jax.random.uniform(jax.random.fold_in(own, axis_at), (parts,), jnp.float32, smallest / len(cuts), high / len(cuts)))
        gain = gain * jnp.repeat(steps, extent[axis_at] // parts).reshape([-1 if axis == axis_at else 1 for axis in range(len(extent))])
    return gain


def setup_inputs(seed: int = 0) -> dict:
    seeds = jax.random.split(jax.random.key(seed), 8)
    density = jnp.clip(jnp.exp(math.log(1.0) - 4.6051702 * jax.random.uniform(seeds[0], (NB, NX, CY), jnp.float32) ** block_scale(seeds[0], (NB, NX, CY), ((0, 8), (1, 64)), -0.2, 0.2)), 0.01, 1.0)
    velocity = jnp.clip(0.02 + 0.32999999 * jax.random.uniform(seeds[1], (2, NX, CY), jnp.float32) ** block_scale(seeds[1], (2, NX, CY), ((1, 512),), -0.2, 0.2), 0.02, 0.35)
    growth = jnp.clip(0.02 + 0.28 * jax.random.uniform(seeds[2], (NX, CY), jnp.float32) ** block_scale(seeds[2], (NX, CY), ((0, 64),), -0.2, 0.2), 0.02, 0.3)
    rate = jnp.clip(jnp.exp(math.log(1.0) - 2.3025851 * jax.random.uniform(seeds[3], (NX, CY), jnp.float32) ** block_scale(seeds[3], (NX, CY), ((0, 64),), -0.2, 0.2)), 0.1, 1.0)
    kernel = jnp.clip(jnp.exp(jax.random.uniform(seeds[4], (NB,), jnp.float32, math.log(0.002), math.log(0.05))), 0.002, 0.05)
    direction = set_ends(jax.random.randint(seeds[5], (NX, CY), 0, 2), jax.random.fold_in(seeds[5], 1), 0, 1).astype(jnp.int32)
    neighbour = set_ends(jax.random.randint(seeds[6], (NX, CY), 0, CY), jax.random.fold_in(seeds[6], 1), 0, CY - 1).astype(jnp.int32)
    return {"density": density, "velocity": velocity, "growth": growth, "rate": rate, "kernel": kernel, "direction": direction, "neighbour": neighbour}


def spectral_birth(block, kernel):
    period = 2 * NB
    spectrum = jnp.fft.rfft(block, n=period, axis=0)
    kernel_spectrum = jnp.fft.rfft(kernel, n=period)
    result = jnp.fft.irfft(spectrum * jnp.conj(kernel_spectrum)[:, None, None], n=period, axis=0)
    return result[:NB].astype(block.dtype)


def reference(density, velocity, growth, rate, kernel, direction, neighbour):
    centres = jnp.arange(NB, dtype=jnp.float32).astype(density.dtype)
    size_factor = (0.5 + 0.5 * (centres + 0.5) / NB)[:, None, None]
    lookup = jnp.broadcast_to(neighbour[None], density.shape).astype(jnp.int32)

    def birth_block(block):
        return spectral_birth(block, kernel)

    for repeat in range(STEPS):
        blocks = density.reshape(NB, NX // CX, CX, CY).transpose(1, 0, 2, 3)
        birth = lax.map(birth_block, blocks).transpose(1, 0, 2, 3).reshape(NB, NX, CY)
        padded = jnp.pad(density, ((0, 0), (1, 1), (0, 0)))
        vertical = jnp.where(direction[None] == 0, padded[:, :-2], padded[:, 2:])
        lateral = jnp.take_along_axis(density, lookup, axis=2)
        lower = jnp.concatenate([jnp.zeros((1, NX, CY), density.dtype), density[:-1]], axis=0)
        density = (density - size_factor * (velocity[0] * (density - vertical) + velocity[1] * (density - lateral))
                   - growth * (density - lower) + rate * birth)
    return density
```

```python
import functools

import jax
import jax.numpy as jnp
from jax import lax
from jax.experimental import pallas as pl
from jax.experimental.pallas import tpu as pltpu
from jax.sharding import PartitionSpec as P

MESH = pl.DeviceIdType.MESH
STEPS = 3
PAD = 8
CHUNK = 64


def split(value):
    high = value.astype(jnp.bfloat16)
    low = (value - high.astype(jnp.float32)).astype(jnp.bfloat16)
    return high, low


def kernel(
    pairs, group, rows, local_bins, bins,
    density, velocity, growth, rate, yields, direction, neighbour,
    out,
    dense, speed, cells_f, cells_i, yield_row,
    sent_rows, sent_cells, n0, n1, n2, n3, mate, cells, table, table_low,
    load_sem, cell_send, cell_recv, row_send, row_recv, mate_send, mate_recv, back_send, back_recv,
):
    c, k = lax.axis_index("cell"), lax.axis_index("bin")
    m, p = c // 2, c % 2

    barrier = pltpu.get_barrier_semaphore()

    def greet(cell, bin_at):
        pl.semaphore_signal(barrier, inc=1, device_id=(cell, bin_at), device_id_type=MESH)

    before, after = (c + 2 * pairs - 1) % (2 * pairs), (c + 1) % (2 * pairs)

    @pl.loop(0, group)
    def _(j):
        @pl.when(jnp.logical_and(p == 0, k < 2))
        def _():
            greet(before, j)

        @pl.when(jnp.logical_and(p == 1, k >= group - 2))
        def _():
            greet(after, j)

    @pl.loop(0, 2 * group)
    def _(i):
        cell, bin_at = 2 * m + i // group, i % group

        @pl.when(jnp.logical_or(cell != c, bin_at != k))
        def _():
            greet(cell, bin_at)

    loads = [
        pltpu.make_async_copy(density, dense, load_sem.at[0]),
        pltpu.make_async_copy(velocity, speed, load_sem.at[1]),
        pltpu.make_async_copy(growth, cells_f.at[0], load_sem.at[2]),
        pltpu.make_async_copy(rate, cells_f.at[1], load_sem.at[3]),
        pltpu.make_async_copy(direction, cells_i.at[0], load_sem.at[4]),
        pltpu.make_async_copy(neighbour, cells_i.at[1], load_sem.at[5]),
        pltpu.make_async_copy(yields, yield_row, load_sem.at[6]),
    ]
    for load in loads:
        load.start()
    for load in loads:
        load.wait()

    for q in range(rows):
        sent_rows[q] = dense[pl.ds(q, local_bins, stride=rows), :]
    sent_cells[0:1] = speed[0]
    sent_cells[1:2] = speed[1]
    sent_cells[2:3] = cells_f[0, pl.ds(k, 1), :]
    sent_cells[3:4] = cells_f[1, pl.ds(k, 1), :]
    sent_cells[4:5] = cells_i[0, pl.ds(k, 1), :].astype(jnp.float32)
    sent_cells[5:6] = cells_i[1, pl.ds(k, 1), :].astype(jnp.float32)
    sent_cells[6:8] = jnp.zeros((2, sent_cells.shape[1]), jnp.float32)

    pl.semaphore_wait(barrier, 2 * group - 1 + 2)

    def target(q, layer):
        core = (q + layer) % 2
        chip = m * group + p * (rows // 2) + jnp.where(
            core == 0, (q + layer) // 2, (q + rows - 1 - layer) // 2 - rows // 2
        )
        chip = (chip + pairs * group) % (pairs * group)
        return 2 * (chip // group) + core, chip % group

    mine = pl.ds(pl.multiple_of(PAD + local_bins * k, PAD), local_bins)

    def row_copy(q, layer):
        cell, bin_at = target(q, layer)
        here = jnp.logical_and(cell == c, bin_at == k)
        remote = pltpu.make_async_remote_copy(
            sent_rows.at[q], n0.at[layer, mine], row_send.at[layer * rows + q], row_recv.at[layer],
            device_id=(cell, bin_at), device_id_type=MESH,
        )
        local = pltpu.make_async_copy(sent_rows.at[q], n0.at[layer, mine], row_recv.at[layer])
        return here, remote, local

    def cell_copy(layer):
        cell, bin_at = target(k, layer)
        here = jnp.logical_and(cell == c, bin_at == k)
        remote = pltpu.make_async_remote_copy(
            sent_cells, cells.at[layer], cell_send.at[layer], cell_recv.at[layer],
            device_id=(cell, bin_at), device_id_type=MESH,
        )
        local = pltpu.make_async_copy(sent_cells, cells.at[layer], cell_recv.at[layer])
        return here, remote, local

    def begin(copies):
        here, remote, local = copies

        @pl.when(jnp.logical_not(here))
        def _():
            remote.start()

        @pl.when(here)
        def _():
            local.start()

    def end(copies):
        here, remote, _ = copies

        @pl.when(jnp.logical_not(here))
        def _():
            remote.wait_send()

    for u, layer in ((0, 1), (1, 2), (2, 3), (0, 3)):
        begin(row_copy(jnp.where(p == 0, u, rows - 1 - u), layer))

    @pl.loop(0, 4 * rows)
    def _(t):
        layer, q = t // rows, (t + k) % rows
        u = jnp.where(p == 0, q, rows - 1 - q)
        far = jnp.logical_and(u < layer, (u + layer) % 2 == 1)

        @pl.when(jnp.logical_not(far))
        def _():
            begin(row_copy(q, layer))

        @pl.when(jnp.logical_and(layer == 0, t < STEPS))
        def _():
            begin(cell_copy(t))

    spread = jnp.broadcast_to(yield_row[...], (bins, bins))
    spread = pltpu.roll(spread, 0, 1, stride=1, stride_axis=0)
    at_b = lax.broadcasted_iota(jnp.int32, (bins, bins), 0)
    at_a = lax.broadcasted_iota(jnp.int32, (bins, bins), 1)
    high, low = split(jnp.where(at_a >= at_b, spread, 0.0))
    table[...] = high
    table_low[...] = low

    zero = jnp.zeros((PAD, n0.shape[-1]), jnp.float32)
    for buffer in (n0, n1, n2, n3):
        for layer in range(buffer.shape[0]):
            buffer[layer, 0:PAD] = zero

    body = pl.ds(PAD, bins)
    mate_id = (2 * m + 1 - p, k)

    def give(source, step):
        copy = pltpu.make_async_remote_copy(
            source.at[0, body], mate.at[step], mate_send.at[step], mate_recv.at[step],
            device_id=mate_id, device_id_type=MESH,
        )
        copy.start()
        return copy

    def arrived(layer):
        pltpu.make_async_copy(n0.at[layer, body], n0.at[layer, body], row_recv.at[layer]).wait()

    gifts = []
    arrived(0)
    gifts.append(give(n0, 0))

    lane = n0.shape[-1]
    offset = lax.broadcasted_iota(jnp.int32, (CHUNK, lane), 0).astype(jnp.float32)
    first_size = 0.5 + 0.5 * (offset + 0.5) / bins

    weights = []
    for layer in range(STEPS):
        pltpu.make_async_copy(cells.at[layer], cells.at[layer], cell_recv.at[layer]).wait()
        row = 2 * (m * group + k) + jnp.where(p == 0, -layer, 1 + layer)
        last = 2 * pairs * rows - 1
        v0, v1 = cells[layer, 0:1], cells[layer, 1:2]
        down = cells[layer, 4:5] == 0.0
        from_below = jnp.where(down, v0, 0.0) * jnp.where(row > 0, 1.0, 0.0)
        from_above = jnp.where(down, 0.0, v0) * jnp.where(row < last, 1.0, 0.0)
        core = jnp.where(p == 0, 1.0, 0.0)
        outer = core * from_below + (1.0 - core) * from_above
        inner = core * from_above + (1.0 - core) * from_below
        weights.append(
            (
                v0 + v1, v1, outer, inner, cells[layer, 2:3], cells[layer, 3:4],
                jnp.broadcast_to(cells[layer, 5:6].astype(jnp.int32), (CHUNK, lane)),
            )
        )

    def births(source, layer):
        high, low = split(source[layer, PAD:])
        both = jnp.dot(
            table[...], jnp.concatenate([high, low], axis=1), preferred_element_type=jnp.float32
        )
        rest = jnp.dot(table_low[...], high, preferred_element_type=jnp.float32)
        return both[:, :lane] + both[:, lane:] + rest

    def advance(source, goal, layer, step, birth):
        total, v1, outer, inner, grow, fragment, lookup = weights[layer]
        for i in range(bins // CHUNK):
            low, high = i * CHUNK, (i + 1) * CHUNK
            n = source[layer, PAD + low : PAD + high]
            lower = source[layer, PAD - 1 + low : PAD - 1 + high]
            outside = source[layer + 1, PAD + low : PAD + high]
            if layer == 0:
                inside = mate[step, low:high]
            else:
                inside = source[layer - 1, PAD + low : PAD + high]
            lateral = jnp.take_along_axis(n, lookup, axis=1, mode="promise_in_bounds")
            size = first_size + 0.5 * low / bins
            moved = total * n - v1 * lateral - outer * outside - inner * inside
            goal[layer, PAD + low : PAD + high] = (
                n - size * moved - grow * (n - lower) + fragment * birth[low:high]
            )

    source = n0
    for step, goal in enumerate((n1, n2, n3)):
        for layer in range(STEPS - step):
            if step == 0:
                arrived(layer + 1)
            birth = births(source, layer)
            if layer == 0:
                gifts[step].wait_recv()
            advance(source, goal, layer, step, birth)
            if layer == 0 and step < STEPS - 1:
                gifts.append(give(goal, step + 1))
        source = goal

    holder = 2 * m + (2 * k + p) // rows
    slot = (2 * k + p) % rows

    def back_copy(j):
        here = jnp.logical_and(holder == c, j == k)
        part = n3.at[0, pl.ds(pl.multiple_of(PAD + local_bins * j, PAD), local_bins)]
        remote = pltpu.make_async_remote_copy(
            part, out.at[slot], back_send.at[j], back_recv,
            device_id=(holder, j), device_id_type=MESH,
        )
        local = pltpu.make_async_copy(part, out.at[slot], back_recv)
        return here, remote, local

    @pl.loop(0, group)
    def _(i):
        begin(back_copy((k + 1 + i) % group))

    for gift in gifts:
        gift.wait_send()
    for layer in range(STEPS):
        end(cell_copy(layer))

    @pl.loop(0, 4 * rows)
    def _(t):
        end(row_copy(t % rows, t // rows))

    @pl.loop(0, group)
    def _(j):
        end(back_copy(j))

    pltpu.make_async_copy(out, out, back_recv).wait()


def on_device(pairs, group, density, velocity, growth, rate, yields, direction, neighbour):
    local_bins, rows, lane = density.shape
    bins = yields.shape[0]
    f32, dma = jnp.float32, pltpu.SemaphoreType.DMA
    padded = PAD + bins
    result = pl.pallas_call(
        functools.partial(kernel, pairs, group, rows, local_bins, bins),
        out_shape=jax.ShapeDtypeStruct((rows, local_bins, lane), f32),
        in_specs=[pl.BlockSpec(memory_space=pl.ANY)] * 7,
        out_specs=pl.BlockSpec(memory_space=pltpu.VMEM),
        scratch_shapes=[
            pltpu.VMEM((local_bins * rows, lane), f32),
            pltpu.VMEM((2, 1, lane), f32),
            pltpu.VMEM((2, rows, lane), f32),
            pltpu.VMEM((2, rows, lane), jnp.int32),
            pltpu.VMEM((1, bins), f32),
            pltpu.VMEM((rows, local_bins, lane), f32),
            pltpu.VMEM((8, lane), f32),
            pltpu.VMEM((STEPS + 1, padded, lane), f32),
            pltpu.VMEM((STEPS, padded, lane), f32),
            pltpu.VMEM((STEPS - 1, padded, lane), f32),
            pltpu.VMEM((1, padded, lane), f32),
            pltpu.VMEM((STEPS, bins, lane), f32),
            pltpu.VMEM((STEPS, 8, lane), f32),
            pltpu.VMEM((bins, bins), jnp.bfloat16),
            pltpu.VMEM((bins, bins), jnp.bfloat16),
            dma((7,)),
            dma((STEPS,)),
            dma((STEPS,)),
            dma((4 * rows,)),
            dma((STEPS + 1,)),
            dma((STEPS,)),
            dma((STEPS,)),
            dma((group,)),
            dma,
        ],
        compiler_params=pltpu.CompilerParams(
            collective_id=0, has_side_effects=True, vmem_limit_bytes=60 * 2**20
        ),
        cost_estimate=pl.CostEstimate(flops=10**9, bytes_accessed=2**21, transcendentals=0),
    )(
        density.reshape(local_bins * rows, lane), velocity, growth, rate, yields.reshape(1, bins),
        direction, neighbour,
    )
    return result.transpose(1, 0, 2)


def solution(mesh):
    return jax.shard_map(
        functools.partial(on_device, mesh.shape["cell"] // 2, mesh.shape["bin"]),
        mesh=mesh,
        in_specs=(
            P("bin", "cell", None),
            P(None, ("cell", "bin"), None),
            P("cell", None),
            P("cell", None),
            P(),
            P("cell", None),
            P("cell", None),
        ),
        out_specs=P("bin", "cell", None),
        check_vma=False,
    )
```

```python
import functools

import jax
import jax.numpy as jnp
from jax import lax
from jax.experimental import pallas as pl
from jax.experimental.pallas import tpu as pltpu
from jax.sharding import PartitionSpec as P

MESH = pl.DeviceIdType.MESH
STEPS = 3
PAD = 8
CHUNK = 64


def split(value):
    high = value.astype(jnp.bfloat16)
    low = (value - high.astype(jnp.float32)).astype(jnp.bfloat16)
    return high, low


def kernel(
    pairs, group, rows, local_bins, bins,
    density, velocity, growth, rate, yields, direction, neighbour,
    out,
    dense, speed, cells_f, cells_i, yield_row,
    sent_rows, sent_cells, back, n0, n1, n2, n3, mate, cells, table, table_low,
    load_sem, cell_send, cell_recv, row_send, row_recv, mate_send, mate_recv, back_send, back_recv,
    call_sem,
):
    c, k = lax.axis_index("cell"), lax.axis_index("bin")
    m, p = c // 2, c % 2

    loads = [
        pltpu.make_async_copy(density, dense, load_sem.at[0]),
        pltpu.make_async_copy(velocity, speed, load_sem.at[1]),
        pltpu.make_async_copy(growth, cells_f.at[0], load_sem.at[2]),
        pltpu.make_async_copy(rate, cells_f.at[1], load_sem.at[3]),
        pltpu.make_async_copy(direction, cells_i.at[0], load_sem.at[4]),
        pltpu.make_async_copy(neighbour, cells_i.at[1], load_sem.at[5]),
        pltpu.make_async_copy(yields, yield_row, load_sem.at[6]),
    ]
    for load in loads:
        load.start()

    barrier = pltpu.get_barrier_semaphore()
    slow_pair = m == 0
    slow = jnp.logical_and(c == 0, k == 0)
    called = jnp.logical_and(
        jnp.logical_and(slow_pair, jnp.logical_not(slow)), jnp.logical_or(p == 0, 2 * k < group)
    )
    beside = jnp.logical_or(
        jnp.logical_and(p == 0, m > 0), jnp.logical_and(p == 1, m < pairs - 1)
    )
    on_edge = jnp.logical_or(
        jnp.logical_and(p == 0, k < 2), jnp.logical_and(p == 1, k >= group - 2)
    )

    def greet(cell, bin_at):
        pl.semaphore_signal(barrier, inc=1, device_id=(cell, bin_at), device_id_type=MESH)

    @pl.when(jnp.logical_and(beside, on_edge))
    def _():
        for j in range(group):
            greet(jnp.where(p == 0, c - 1, c + 1), j)

    @pl.when(jnp.logical_not(slow))
    def _():
        for i in range(2 * group):
            cell, bin_at = 2 * m + i // group, i % group

            @pl.when(jnp.logical_or(cell != c, bin_at != k))
            def _():
                greet(cell, bin_at)

    for load in loads:
        load.wait()

    for q in range(rows):
        sent_rows[q] = dense[pl.ds(q, local_bins, stride=rows), :]
    sent_cells[0:1] = speed[0]
    sent_cells[1:2] = speed[1]
    sent_cells[2:3] = cells_f[0, pl.ds(k, 1), :]
    sent_cells[3:4] = cells_f[1, pl.ds(k, 1), :]
    sent_cells[4:5] = cells_i[0, pl.ds(k, 1), :].astype(jnp.float32)
    sent_cells[5:6] = cells_i[1, pl.ds(k, 1), :].astype(jnp.float32)
    sent_cells[6:8] = jnp.zeros((2, sent_cells.shape[1]), jnp.float32)

    waits = 2 * group - 1 + jnp.where(beside, 2, 0)
    pl.semaphore_wait(
        barrier, waits - jnp.where(jnp.logical_and(slow_pair, jnp.logical_not(slow)), 1, 0)
    )

    @pl.when(slow)
    def _():
        for i in range(1, 2 * group):
            if i < group + group // 2:
                pl.semaphore_signal(
                    call_sem, inc=1, device_id=(i // group, i % group), device_id_type=MESH
                )

    def target(q, layer):
        core = (q + layer) % 2
        chip = m * group + p * (rows // 2) + jnp.where(
            core == 0, (q + layer) // 2, (q + rows - 1 - layer) // 2 - rows // 2
        )
        return 2 * (chip // group) + core, chip % group

    mine = pl.ds(pl.multiple_of(PAD + local_bins * k, PAD), local_bins)

    def row_copy(q, layer):
        cell, bin_at = target(q, layer)
        here = jnp.logical_and(cell == c, bin_at == k)
        remote = pltpu.make_async_remote_copy(
            sent_rows.at[q], n0.at[layer, mine], row_send.at[layer * rows + q], row_recv.at[layer],
            device_id=(cell, bin_at), device_id_type=MESH,
        )
        local = pltpu.make_async_copy(sent_rows.at[q], n0.at[layer, mine], row_recv.at[layer])
        return here, remote, local

    def cell_copy(layer):
        cell, bin_at = target(k, layer)
        here = jnp.logical_and(cell == c, bin_at == k)
        remote = pltpu.make_async_remote_copy(
            sent_cells, cells.at[layer], cell_send.at[layer], cell_recv.at[layer],
            device_id=(cell, bin_at), device_id_type=MESH,
        )
        local = pltpu.make_async_copy(sent_cells, cells.at[layer], cell_recv.at[layer])
        return here, remote, local

    def begin(copies):
        here, remote, local = copies

        @pl.when(jnp.logical_not(here))
        def _():
            remote.start()

        @pl.when(here)
        def _():
            local.start()

    def end(copies):
        here, remote, _ = copies

        @pl.when(jnp.logical_not(here))
        def _():
            remote.wait_send()

    def is_far(q, layer):
        u = jnp.where(p == 0, q, rows - 1 - q)
        return jnp.logical_and(u < layer, (u + layer) % 2 == 1)

    @pl.when(beside)
    def _():
        for u, layer in ((0, 1), (1, 2), (2, 3), (0, 3)):
            begin(row_copy(jnp.where(p == 0, u, rows - 1 - u), layer))

    @pl.loop(0, 4 * rows)
    def _(t):
        layer, q = t // rows, (t + k) % rows
        later = jnp.logical_and(jnp.logical_and(called, p == 0), t + k == rows * jnp.where(t < rows, 1, 0))

        @pl.when(jnp.logical_not(jnp.logical_or(is_far(q, layer), later)))
        def _():
            begin(row_copy(q, layer))

        @pl.when(jnp.logical_and(t < STEPS, jnp.logical_or(beside, jnp.logical_not(is_far(k, t)))))
        def _():
            begin(cell_copy(t))

    spread = jnp.broadcast_to(yield_row[...], (bins, bins))
    spread = pltpu.roll(spread, 0, 1, stride=1, stride_axis=0)
    at_b = lax.broadcasted_iota(jnp.int32, (bins, bins), 0)
    at_a = lax.broadcasted_iota(jnp.int32, (bins, bins), 1)
    high, low = split(jnp.where(at_a >= at_b, spread, 0.0))
    table[...] = high
    table_low[...] = low

    zero = jnp.zeros((PAD, n0.shape[-1]), jnp.float32)
    for buffer in (n0, n1, n2, n3):
        for layer in range(buffer.shape[0]):
            buffer[layer, 0:PAD] = zero

    body = pl.ds(PAD, bins)
    mate_id = (2 * m + 1 - p, k)

    def give(source, step):
        copy = pltpu.make_async_remote_copy(
            source.at[0, body], mate.at[step], mate_send.at[step], mate_recv.at[step],
            device_id=mate_id, device_id_type=MESH,
        )
        copy.start()
        return copy

    last = 2 * pairs * rows - 1

    def row_of(layer):
        return 2 * (m * group + k) + jnp.where(p == 0, -layer, 1 + layer)

    def is_row(layer):
        return jnp.logical_and(row_of(layer) >= 0, row_of(layer) <= last)

    def arrived(layer):
        @pl.when(is_row(layer))
        def _():
            pltpu.make_async_copy(n0.at[layer, body], n0.at[layer, body], row_recv.at[layer]).wait()

    for layer in range(1, STEPS + 1):
        @pl.when(jnp.logical_not(is_row(layer)))
        def _():
            n0[layer, PAD:] = jnp.zeros((bins, n0.shape[-1]), jnp.float32)
            if layer < STEPS:
                cells[layer] = jnp.zeros(cells.shape[1:], jnp.float32)

    @pl.when(called)
    def _():
        pl.semaphore_wait(call_sem, 1)

        @pl.when(p == 0)
        def _():
            begin(row_copy(0, 0))

    gifts = []
    arrived(0)
    gifts.append(give(n0, 0))

    lane = n0.shape[-1]
    offset = lax.broadcasted_iota(jnp.int32, (CHUNK, lane), 0).astype(jnp.float32)
    first_size = 0.5 + 0.5 * (offset + 0.5) / bins

    weights = []
    for layer in range(STEPS):
        @pl.when(is_row(layer))
        def _():
            pltpu.make_async_copy(cells.at[layer], cells.at[layer], cell_recv.at[layer]).wait()

        row = row_of(layer)
        v0, v1 = cells[layer, 0:1], cells[layer, 1:2]
        down = cells[layer, 4:5] == 0.0
        from_below = jnp.where(down, v0, 0.0) * jnp.where(row > 0, 1.0, 0.0)
        from_above = jnp.where(down, 0.0, v0) * jnp.where(row < last, 1.0, 0.0)
        core = jnp.where(p == 0, 1.0, 0.0)
        outer = core * from_below + (1.0 - core) * from_above
        inner = core * from_above + (1.0 - core) * from_below
        weights.append(
            (
                v0 + v1, v1, outer, inner, cells[layer, 2:3], cells[layer, 3:4],
                jnp.broadcast_to(cells[layer, 5:6].astype(jnp.int32), (CHUNK, lane)),
            )
        )

    def births(source, layer):
        high, low = split(source[layer, PAD:])
        both = jnp.dot(
            table[...], jnp.concatenate([high, low], axis=1), preferred_element_type=jnp.float32
        )
        rest = jnp.dot(table_low[...], high, preferred_element_type=jnp.float32)
        return both[:, :lane] + both[:, lane:] + rest

    def advance(source, goal, layer, step, birth):
        total, v1, outer, inner, grow, fragment, lookup = weights[layer]
        for i in range(bins // CHUNK):
            low, high = i * CHUNK, (i + 1) * CHUNK
            n = source[layer, PAD + low : PAD + high]
            lower = source[layer, PAD - 1 + low : PAD - 1 + high]
            outside = source[layer + 1, PAD + low : PAD + high]
            if layer == 0:
                inside = mate[step, low:high]
            else:
                inside = source[layer - 1, PAD + low : PAD + high]
            lateral = jnp.take_along_axis(n, lookup, axis=1, mode="promise_in_bounds")
            size = first_size + 0.5 * low / bins
            moved = total * n - v1 * lateral - outer * outside - inner * inside
            goal[layer, PAD + low : PAD + high] = (
                n - size * moved - grow * (n - lower) + fragment * birth[low:high]
            )

    source = n0
    for step, goal in enumerate((n1, n2, n3)):
        for layer in range(STEPS - step):
            birth = births(source, layer)
            if step == 0:
                arrived(layer + 1)
            if layer == 0:
                gifts[step].wait_recv()
            advance(source, goal, layer, step, birth)
            if layer == 0 and step < STEPS - 1:
                gifts.append(give(goal, step + 1))
        source = goal

    holder = 2 * m + (2 * k + p) // rows
    slot = (2 * k + p) % rows

    def back_copy(j):
        here = jnp.logical_and(holder == c, j == k)
        part = n3.at[0, pl.ds(pl.multiple_of(PAD + local_bins * j, PAD), local_bins)]
        remote = pltpu.make_async_remote_copy(
            part, back.at[slot], back_send.at[j], back_recv,
            device_id=(holder, j), device_id_type=MESH,
        )
        local = pltpu.make_async_copy(part, back.at[slot], back_recv)
        return here, remote, local

    @pl.loop(0, group)
    def _(i):
        begin(back_copy((k + 1 + i) % group))

    for gift in gifts:
        gift.wait_send()
    for layer in range(STEPS):
        @pl.when(jnp.logical_or(beside, jnp.logical_not(is_far(k, layer))))
        def _():
            end(cell_copy(layer))

    @pl.loop(0, 4 * rows)
    def _(t):
        @pl.when(jnp.logical_or(beside, jnp.logical_not(is_far(t % rows, t // rows))))
        def _():
            end(row_copy(t % rows, t // rows))

    pltpu.make_async_copy(back, back, back_recv).wait()
    for q in range(rows):
        out[pl.ds(q, local_bins, stride=rows), :] = back[q]

    @pl.loop(0, group)
    def _(j):
        end(back_copy(j))


def on_device(pairs, group, density, velocity, growth, rate, yields, direction, neighbour):
    local_bins, rows, lane = density.shape
    bins = yields.shape[0]
    f32, dma = jnp.float32, pltpu.SemaphoreType.DMA
    padded = PAD + bins
    result = pl.pallas_call(
        functools.partial(kernel, pairs, group, rows, local_bins, bins),
        out_shape=jax.ShapeDtypeStruct((local_bins * rows, lane), f32),
        in_specs=[pl.BlockSpec(memory_space=pltpu.HBM)] * 7,
        out_specs=pl.BlockSpec(memory_space=pltpu.VMEM),
        scratch_shapes=[
            pltpu.VMEM((local_bins * rows, lane), f32),
            pltpu.VMEM((2, 1, lane), f32),
            pltpu.VMEM((2, rows, lane), f32),
            pltpu.VMEM((2, rows, lane), jnp.int32),
            pltpu.VMEM((1, bins), f32),
            pltpu.VMEM((rows, local_bins, lane), f32),
            pltpu.VMEM((8, lane), f32),
            pltpu.VMEM((rows, local_bins, lane), f32),
            pltpu.VMEM((STEPS + 1, padded, lane), f32),
            pltpu.VMEM((STEPS, padded, lane), f32),
            pltpu.VMEM((STEPS - 1, padded, lane), f32),
            pltpu.VMEM((1, padded, lane), f32),
            pltpu.VMEM((STEPS, bins, lane), f32),
            pltpu.VMEM((STEPS, 8, lane), f32),
            pltpu.VMEM((bins, bins), jnp.bfloat16),
            pltpu.VMEM((bins, bins), jnp.bfloat16),
            dma((7,)),
            dma((STEPS,)),
            dma((STEPS,)),
            dma((4 * rows,)),
            dma((STEPS + 1,)),
            dma((STEPS,)),
            dma((STEPS,)),
            dma((group,)),
            dma,
            pltpu.SemaphoreType.REGULAR,
        ],
        compiler_params=pltpu.CompilerParams(
            collective_id=0, has_side_effects=True, vmem_limit_bytes=60 * 2**20
        ),
        cost_estimate=pl.CostEstimate(flops=10**9, bytes_accessed=2**21, transcendentals=0),
    )(
        density.reshape(local_bins * rows, lane), velocity, growth, rate, yields.reshape(1, bins),
        direction, neighbour,
    )
    return result.reshape(density.shape)


def solution(mesh):
    return jax.shard_map(
        functools.partial(on_device, mesh.shape["cell"] // 2, mesh.shape["bin"]),
        mesh=mesh,
        in_specs=(
            P("bin", "cell", None),
            P(None, ("cell", "bin"), None),
            P("cell", None),
            P("cell", None),
            P(),
            P("cell", None),
            P("cell", None),
        ),
        out_specs=P("bin", "cell", None),
        check_vma=False,
    )
```

```python
import functools

import jax
import jax.numpy as jnp
from jax import lax
from jax.experimental import pallas as pl
from jax.experimental.pallas import tpu as pltpu
from jax.sharding import PartitionSpec as P

MESH = pl.DeviceIdType.MESH
STEPS = 3
PAD = 8
CHUNK = 64


def split(value):
    high = value.astype(jnp.bfloat16)
    low = (value - high.astype(jnp.float32)).astype(jnp.bfloat16)
    return high, low


def kernel(
    pairs, group, rows, local_bins, bins,
    density, velocity, growth, rate, yields, direction, neighbour,
    out,
    dense, speed, cells_f, cells_i, yield_row,
    sent_rows, sent_cells, back, n0, n1, n2, n3, mate, cells, table, table_low,
    load_sem, cell_send, cell_recv, row_send, row_recv, mate_send, mate_recv, back_send, back_recv,
    call_sem,
):
    c, k = lax.axis_index("cell"), lax.axis_index("bin")
    m, p = c // 2, c % 2

    loads = [
        pltpu.make_async_copy(density, dense, load_sem.at[0]),
        pltpu.make_async_copy(velocity, speed, load_sem.at[1]),
        pltpu.make_async_copy(growth, cells_f.at[0], load_sem.at[2]),
        pltpu.make_async_copy(rate, cells_f.at[1], load_sem.at[3]),
        pltpu.make_async_copy(direction, cells_i.at[0], load_sem.at[4]),
        pltpu.make_async_copy(neighbour, cells_i.at[1], load_sem.at[5]),
        pltpu.make_async_copy(yields, yield_row, load_sem.at[6]),
    ]
    for load in loads:
        load.start()

    barrier = pltpu.get_barrier_semaphore()
    slow_pair = m == 0
    slow = jnp.logical_and(c == 0, k == 0)
    called = jnp.logical_and(
        jnp.logical_and(slow_pair, jnp.logical_not(slow)), jnp.logical_or(p == 0, 2 * k < group)
    )
    beside = jnp.logical_or(
        jnp.logical_and(p == 0, m > 0), jnp.logical_and(p == 1, m < pairs - 1)
    )
    on_edge = jnp.logical_or(
        jnp.logical_and(p == 0, k < 2), jnp.logical_and(p == 1, k >= group - 2)
    )

    def greet(cell, bin_at):
        pl.semaphore_signal(barrier, inc=1, device_id=(cell, bin_at), device_id_type=MESH)

    @pl.when(jnp.logical_and(beside, on_edge))
    def _():
        for j in range(group):
            greet(jnp.where(p == 0, c - 1, c + 1), j)

    @pl.when(jnp.logical_not(slow))
    def _():
        for i in range(2 * group):
            cell, bin_at = 2 * m + i // group, i % group

            @pl.when(jnp.logical_or(cell != c, bin_at != k))
            def _():
                greet(cell, bin_at)

    for load in loads:
        load.wait()

    for q in range(rows):
        sent_rows[q] = dense[pl.ds(q, local_bins, stride=rows), :]
    sent_cells[0:1] = speed[0]
    sent_cells[1:2] = speed[1]
    sent_cells[2:3] = cells_f[0, pl.ds(k, 1), :]
    sent_cells[3:4] = cells_f[1, pl.ds(k, 1), :]
    sent_cells[4:5] = cells_i[0, pl.ds(k, 1), :].astype(jnp.float32)
    sent_cells[5:6] = cells_i[1, pl.ds(k, 1), :].astype(jnp.float32)
    sent_cells[6:8] = jnp.zeros((2, sent_cells.shape[1]), jnp.float32)

    waits = 2 * group - 1 + jnp.where(beside, 2, 0)
    pl.semaphore_wait(
        barrier, waits - jnp.where(jnp.logical_and(slow_pair, jnp.logical_not(slow)), 1, 0)
    )

    @pl.when(slow)
    def _():
        for i in range(1, 2 * group):
            if i < group + group // 2:
                pl.semaphore_signal(
                    call_sem, inc=1, device_id=(i // group, i % group), device_id_type=MESH
                )

    def target(q, layer):
        core = (q + layer) % 2
        chip = m * group + p * (rows // 2) + jnp.where(
            core == 0, (q + layer) // 2, (q + rows - 1 - layer) // 2 - rows // 2
        )
        return 2 * (chip // group) + core, chip % group

    mine = pl.ds(pl.multiple_of(PAD + local_bins * k, PAD), local_bins)

    def row_copy(q, layer):
        cell, bin_at = target(q, layer)
        here = jnp.logical_and(cell == c, bin_at == k)
        remote = pltpu.make_async_remote_copy(
            sent_rows.at[q], n0.at[layer, mine], row_send.at[layer * rows + q], row_recv.at[layer],
            device_id=(cell, bin_at), device_id_type=MESH,
        )
        local = pltpu.make_async_copy(sent_rows.at[q], n0.at[layer, mine], row_recv.at[layer])
        return here, remote, local

    def cell_copy(layer):
        cell, bin_at = target(k, layer)
        here = jnp.logical_and(cell == c, bin_at == k)
        remote = pltpu.make_async_remote_copy(
            sent_cells, cells.at[layer], cell_send.at[layer], cell_recv.at[layer],
            device_id=(cell, bin_at), device_id_type=MESH,
        )
        local = pltpu.make_async_copy(sent_cells, cells.at[layer], cell_recv.at[layer])
        return here, remote, local

    def begin(copies):
        here, remote, local = copies

        @pl.when(jnp.logical_not(here))
        def _():
            remote.start()

        @pl.when(here)
        def _():
            local.start()

    def end(copies):
        here, remote, _ = copies

        @pl.when(jnp.logical_not(here))
        def _():
            remote.wait_send()

    def is_far(q, layer):
        u = jnp.where(p == 0, q, rows - 1 - q)
        return jnp.logical_and(u < layer, (u + layer) % 2 == 1)

    @pl.when(beside)
    def _():
        for u, layer in ((0, 1), (1, 2), (2, 3), (0, 3)):
            begin(row_copy(jnp.where(p == 0, u, rows - 1 - u), layer))

    @pl.loop(0, 4 * rows)
    def _(t):
        layer, q = t // rows, (t + k) % rows
        later = jnp.logical_and(jnp.logical_and(called, p == 0), t + k == rows * jnp.where(t < rows, 1, 0))

        @pl.when(jnp.logical_not(jnp.logical_or(is_far(q, layer), later)))
        def _():
            begin(row_copy(q, layer))

        @pl.when(jnp.logical_and(t < STEPS, jnp.logical_or(beside, jnp.logical_not(is_far(k, t)))))
        def _():
            begin(cell_copy(t))

    spread = jnp.broadcast_to(yield_row[...], (bins, bins))
    spread = pltpu.roll(spread, 0, 1, stride=1, stride_axis=0)
    at_b = lax.broadcasted_iota(jnp.int32, (bins, bins), 0)
    at_a = lax.broadcasted_iota(jnp.int32, (bins, bins), 1)
    high, low = split(jnp.where(at_a >= at_b, spread, 0.0))
    table[...] = high
    table_low[...] = low

    zero = jnp.zeros((PAD, n0.shape[-1]), jnp.float32)
    for buffer in (n0, n1, n2, n3):
        for layer in range(buffer.shape[0]):
            buffer[layer, 0:PAD] = zero

    body = pl.ds(PAD, bins)
    mate_id = (2 * m + 1 - p, k)

    def give(source, step):
        copy = pltpu.make_async_remote_copy(
            source.at[0, body], mate.at[step], mate_send.at[step], mate_recv.at[step],
            device_id=mate_id, device_id_type=MESH,
        )
        copy.start()
        return copy

    last = 2 * pairs * rows - 1

    def row_of(layer):
        return 2 * (m * group + k) + jnp.where(p == 0, -layer, 1 + layer)

    def is_row(layer):
        return jnp.logical_and(row_of(layer) >= 0, row_of(layer) <= last)

    def arrived(layer):
        @pl.when(is_row(layer))
        def _():
            pltpu.make_async_copy(n0.at[layer, body], n0.at[layer, body], row_recv.at[layer]).wait()

    for layer in range(1, STEPS + 1):
        @pl.when(jnp.logical_not(is_row(layer)))
        def _():
            n0[layer, PAD:] = jnp.zeros((bins, n0.shape[-1]), jnp.float32)
            if layer < STEPS:
                cells[layer] = jnp.zeros(cells.shape[1:], jnp.float32)

    @pl.when(called)
    def _():
        pl.semaphore_wait(call_sem, 1)

        @pl.when(p == 0)
        def _():
            begin(row_copy(0, 0))

    gifts = []
    arrived(0)
    gifts.append(give(n0, 0))

    lane = n0.shape[-1]
    offset = lax.broadcasted_iota(jnp.int32, (CHUNK, lane), 0).astype(jnp.float32)
    first_size = 0.5 + 0.5 * (offset + 0.5) / bins

    weights = []
    for layer in range(STEPS):
        @pl.when(is_row(layer))
        def _():
            pltpu.make_async_copy(cells.at[layer], cells.at[layer], cell_recv.at[layer]).wait()

        row = row_of(layer)
        v0, v1 = cells[layer, 0:1], cells[layer, 1:2]
        down = cells[layer, 4:5] == 0.0
        from_below = jnp.where(down, v0, 0.0) * jnp.where(row > 0, 1.0, 0.0)
        from_above = jnp.where(down, 0.0, v0) * jnp.where(row < last, 1.0, 0.0)
        core = jnp.where(p == 0, 1.0, 0.0)
        outer = core * from_below + (1.0 - core) * from_above
        inner = core * from_above + (1.0 - core) * from_below
        weights.append(
            (
                v0 + v1, v1, outer, inner, cells[layer, 2:3], cells[layer, 3:4],
                jnp.broadcast_to(cells[layer, 5:6].astype(jnp.int32), (CHUNK, lane)),
            )
        )

    def births(source, layer):
        high, low = split(source[layer, PAD:])
        both = jnp.dot(
            table[...], jnp.concatenate([high, low], axis=1), preferred_element_type=jnp.float32
        )
        rest = jnp.dot(table_low[...], high, preferred_element_type=jnp.float32)
        return both[:, :lane] + both[:, lane:] + rest

    def advance(source, goal, layer, step, birth):
        total, v1, outer, inner, grow, fragment, lookup = weights[layer]
        for i in range(bins // CHUNK):
            low, high = i * CHUNK, (i + 1) * CHUNK
            n = source[layer, PAD + low : PAD + high]
            lower = source[layer, PAD - 1 + low : PAD - 1 + high]
            outside = source[layer + 1, PAD + low : PAD + high]
            if layer == 0:
                inside = mate[step, low:high]
            else:
                inside = source[layer - 1, PAD + low : PAD + high]
            lateral = jnp.take_along_axis(n, lookup, axis=1, mode="promise_in_bounds")
            size = first_size + 0.5 * low / bins
            moved = total * n - v1 * lateral - outer * outside - inner * inside
            goal[layer, PAD + low : PAD + high] = (
                n - size * moved - grow * (n - lower) + fragment * birth[low:high]
            )

    source = n0
    for step, goal in enumerate((n1, n2, n3)):
        for layer in range(STEPS - step):
            birth = births(source, layer)
            if step == 0:
                arrived(layer + 1)
            if layer == 0:
                gifts[step].wait_recv()
            advance(source, goal, layer, step, birth)
            if layer == 0 and step < STEPS - 1:
                gifts.append(give(goal, step + 1))
        source = goal

    holder = 2 * m + (2 * k + p) // rows
    slot = (2 * k + p) % rows

    def back_copy(j):
        here = jnp.logical_and(holder == c, j == k)
        part = n3.at[0, pl.ds(pl.multiple_of(PAD + local_bins * j, PAD), local_bins)]
        remote = pltpu.make_async_remote_copy(
            part, back.at[slot], back_send.at[j], back_recv,
            device_id=(holder, j), device_id_type=MESH,
        )
        local = pltpu.make_async_copy(part, back.at[slot], back_recv)
        return here, remote, local

    @pl.loop(0, group)
    def _(i):
        begin(back_copy((k + 1 + i) % group))

    for gift in gifts:
        gift.wait_send()
    for layer in range(STEPS):
        @pl.when(jnp.logical_or(beside, jnp.logical_not(is_far(k, layer))))
        def _():
            end(cell_copy(layer))

    @pl.loop(0, 4 * rows)
    def _(t):
        @pl.when(jnp.logical_or(beside, jnp.logical_not(is_far(t % rows, t // rows))))
        def _():
            end(row_copy(t % rows, t // rows))

    pltpu.make_async_copy(back, back, back_recv).wait()
    for q in range(rows):
        out[pl.ds(q, local_bins, stride=rows), :] = back[q]

    @pl.loop(0, group)
    def _(j):
        end(back_copy(j))


def on_device(pairs, group, density, velocity, growth, rate, yields, direction, neighbour):
    local_bins, rows, lane = density.shape
    bins = yields.shape[0]
    f32, dma = jnp.float32, pltpu.SemaphoreType.DMA
    padded = PAD + bins
    result = pl.pallas_call(
        functools.partial(kernel, pairs, group, rows, local_bins, bins),
        out_shape=pltpu.VMEM((local_bins * rows, lane), f32),
        in_specs=[pl.BlockSpec(memory_space=pltpu.HBM)] * 7,
        out_specs=pl.BlockSpec(memory_space=pltpu.VMEM),
        scratch_shapes=[
            pltpu.VMEM((local_bins * rows, lane), f32),
            pltpu.VMEM((2, 1, lane), f32),
            pltpu.VMEM((2, rows, lane), f32),
            pltpu.VMEM((2, rows, lane), jnp.int32),
            pltpu.VMEM((1, bins), f32),
            pltpu.VMEM((rows, local_bins, lane), f32),
            pltpu.VMEM((8, lane), f32),
            pltpu.VMEM((rows, local_bins, lane), f32),
            pltpu.VMEM((STEPS + 1, padded, lane), f32),
            pltpu.VMEM((STEPS, padded, lane), f32),
            pltpu.VMEM((STEPS - 1, padded, lane), f32),
            pltpu.VMEM((1, padded, lane), f32),
            pltpu.VMEM((STEPS, bins, lane), f32),
            pltpu.VMEM((STEPS, 8, lane), f32),
            pltpu.VMEM((bins, bins), jnp.bfloat16),
            pltpu.VMEM((bins, bins), jnp.bfloat16),
            dma((7,)),
            dma((STEPS,)),
            dma((STEPS,)),
            dma((4 * rows,)),
            dma((STEPS + 1,)),
            dma((STEPS,)),
            dma((STEPS,)),
            dma((group,)),
            dma,
            pltpu.SemaphoreType.REGULAR,
        ],
        compiler_params=pltpu.CompilerParams(
            collective_id=0, has_side_effects=True, vmem_limit_bytes=60 * 2**20
        ),
        cost_estimate=pl.CostEstimate(flops=10**9, bytes_accessed=2**21, transcendentals=0),
    )(
        density.reshape(local_bins * rows, lane), velocity, growth, rate, yields.reshape(1, bins),
        direction, neighbour,
    )
    return result.reshape(density.shape)


def solution(mesh):
    return jax.shard_map(
        functools.partial(on_device, mesh.shape["cell"] // 2, mesh.shape["bin"]),
        mesh=mesh,
        in_specs=(
            P("bin", "cell", None),
            P(None, ("cell", "bin"), None),
            P("cell", None),
            P("cell", None),
            P(),
            P("cell", None),
            P("cell", None),
        ),
        out_specs=P("bin", "cell", None),
        check_vma=False,
    )
```

```python
import functools

import jax
import jax.numpy as jnp
from jax import lax
from jax.experimental import pallas as pl
from jax.experimental.pallas import tpu as pltpu
from jax.sharding import PartitionSpec as P

MESH = pl.DeviceIdType.MESH
STEPS = 3
PAD = 8
CHUNK = 64


def split(value):
    high = value.astype(jnp.bfloat16)
    low = (value - high.astype(jnp.float32)).astype(jnp.bfloat16)
    return high, low


def kernel(
    pairs, group, rows, local_bins, bins,
    density, velocity, growth, rate, yields, direction, neighbour,
    out,
    dense, speed, cells_f, cells_i, yield_row,
    sent_rows, sent_cells, back, n0, n1, n2, n3, cells, table, table_low,
    load_sem, cell_send, cell_recv, row_send, row_recv, mate_send, mate_recv, back_send, back_recv,
    mate_cell_send, mate_cell_recv, call_sem,
):
    c, k = lax.axis_index("cell"), lax.axis_index("bin")
    m, p = c // 2, c % 2

    loads = [
        pltpu.make_async_copy(density, dense, load_sem.at[0]),
        pltpu.make_async_copy(velocity, speed, load_sem.at[1]),
        pltpu.make_async_copy(growth, cells_f.at[0], load_sem.at[2]),
        pltpu.make_async_copy(rate, cells_f.at[1], load_sem.at[3]),
        pltpu.make_async_copy(direction, cells_i.at[0], load_sem.at[4]),
        pltpu.make_async_copy(neighbour, cells_i.at[1], load_sem.at[5]),
        pltpu.make_async_copy(yields, yield_row, load_sem.at[6]),
    ]
    for load in loads:
        load.start()

    barrier = pltpu.get_barrier_semaphore()
    slow_pair = m == 0
    slow = jnp.logical_and(c == 0, k == 0)
    called = jnp.logical_and(
        jnp.logical_and(slow_pair, jnp.logical_not(slow)), jnp.logical_or(p == 0, 2 * k < group)
    )
    beside = jnp.logical_or(
        jnp.logical_and(p == 0, m > 0), jnp.logical_and(p == 1, m < pairs - 1)
    )
    on_edge = jnp.logical_or(
        jnp.logical_and(p == 0, k < 2), jnp.logical_and(p == 1, k >= group - 2)
    )

    def greet(cell, bin_at):
        pl.semaphore_signal(barrier, inc=1, device_id=(cell, bin_at), device_id_type=MESH)

    @pl.when(jnp.logical_and(beside, on_edge))
    def _():
        for j in range(group):
            greet(jnp.where(p == 0, c - 1, c + 1), j)

    @pl.when(jnp.logical_not(slow))
    def _():
        for i in range(2 * group):
            cell, bin_at = 2 * m + i // group, i % group

            @pl.when(jnp.logical_or(cell != c, bin_at != k))
            def _():
                greet(cell, bin_at)

    @pl.when(slow)
    def _():
        pl.semaphore_wait(barrier, 2 * group - 1)
        for i in range(1, group + group // 2):
            pl.semaphore_signal(
                call_sem, inc=1, device_id=(i // group, i % group), device_id_type=MESH
            )

    for load in loads:
        load.wait()

    for q in range(rows):
        sent_rows[q] = dense[pl.ds(q, local_bins, stride=rows), :]
    sent_cells[0:1] = speed[0]
    sent_cells[1:2] = speed[1]
    sent_cells[2:3] = cells_f[0, pl.ds(k, 1), :]
    sent_cells[3:4] = cells_f[1, pl.ds(k, 1), :]
    sent_cells[4:5] = cells_i[0, pl.ds(k, 1), :].astype(jnp.float32)
    sent_cells[5:6] = cells_i[1, pl.ds(k, 1), :].astype(jnp.float32)
    sent_cells[6:8] = jnp.zeros((2, sent_cells.shape[1]), jnp.float32)

    @pl.when(jnp.logical_not(slow))
    def _():
        pl.semaphore_wait(
            barrier, 2 * group - 1 + jnp.where(beside, 2, 0) - jnp.where(slow_pair, 1, 0)
        )

    mine = pl.ds(pl.multiple_of(PAD + local_bins * k, PAD), local_bins)
    first_chip = p * (rows // 2)

    def target(q, layer):
        half = lax.div(q, 2)
        odd = q - 2 * half
        shift = (layer + 1) // 2
        core = odd if layer % 2 == 0 else 1 - odd
        return core, first_chip + half + shift - 2 * shift * core

    def cases(core, chip):
        near = jnp.logical_and(chip >= 0, chip < group)
        here = jnp.logical_and(chip == k, core == p)
        return jnp.logical_and(near, jnp.logical_not(here)), here

    def remote_row(q, layer, cell, bin_at):
        return pltpu.make_async_remote_copy(
            sent_rows.at[q], n0.at[STEPS - layer, mine], row_send.at[layer * rows + q],
            row_recv.at[layer], device_id=(cell, bin_at), device_id_type=MESH,
        )

    def remote_cell(layer, cell, bin_at):
        return pltpu.make_async_remote_copy(
            sent_cells, cells.at[STEPS - layer], cell_send.at[layer], cell_recv.at[layer],
            device_id=(cell, bin_at), device_id_type=MESH,
        )

    far_cell = jnp.where(p == 0, c - 1, c + 1)
    far_first = jnp.where(p == 0, group, -group)
    far = []
    for u, layer in ((0, 1), (1, 2), (2, 3), (0, 3)):
        far.append((jnp.where(p == 0, u, rows - 1 - u), layer))

    @pl.when(beside)
    def _():
        for q, layer in far:
            _, chip = target(q, layer)
            remote_row(q, layer, far_cell, chip + far_first).start()

    called_0 = jnp.logical_and(called, p == 0)
    for layer in range(STEPS + 1):
        if layer < STEPS:
            core, chip = target(k, layer)
            go, here = cases(core, chip)
            outside = jnp.logical_or(chip < 0, chip >= group)

            @pl.when(go)
            def _():
                remote_cell(layer, 2 * m + core, chip).start()

            @pl.when(here)
            def _():
                pltpu.make_async_copy(
                    sent_cells, cells.at[STEPS - layer], cell_recv.at[layer]
                ).start()

            @pl.when(jnp.logical_and(outside, beside))
            def _():
                remote_cell(layer, far_cell, chip + far_first).start()

        @pl.loop(0, rows)
        def _(t):
            q = t + k
            q = jnp.where(q >= rows, q - rows, q)
            core, chip = target(q, layer)
            go, here = cases(core, chip)
            if layer == 0:
                go = jnp.logical_and(go, jnp.logical_not(jnp.logical_and(called_0, q == 0)))

            @pl.when(go)
            def _():
                remote_row(q, layer, 2 * m + core, chip).start()

            @pl.when(here)
            def _():
                pltpu.make_async_copy(
                    sent_rows.at[q], n0.at[STEPS - layer, mine], row_recv.at[layer]
                ).start()

    spread = jnp.broadcast_to(yield_row[...], (bins, bins))
    spread = pltpu.roll(spread, 0, 1, stride=1, stride_axis=0)
    at_b = lax.broadcasted_iota(jnp.int32, (bins, bins), 0)
    at_a = lax.broadcasted_iota(jnp.int32, (bins, bins), 1)
    high, low = split(jnp.where(at_a >= at_b, spread, 0.0))
    table[...] = high
    table_low[...] = low

    lane = n0.shape[-1]
    zero = jnp.zeros((PAD, lane), jnp.float32)
    for buffer in (n0, n1, n2, n3):
        for place in range(buffer.shape[0]):
            buffer[place, 0:PAD] = zero

    body = pl.ds(PAD, bins)
    mate_id = (2 * m + 1 - p, k)
    first = 2 * (m * group + k)
    last = 2 * pairs * rows - 1

    def row_at(place):
        return first + jnp.where(p == 0, place - STEPS, STEPS + 1 - place)

    def is_row(layer):
        row = row_at(STEPS - layer)
        return jnp.logical_and(row >= 0, row <= last)

    for layer in range(1, STEPS + 1):
        @pl.when(jnp.logical_not(is_row(layer)))
        def _():
            n0[STEPS - layer, PAD:] = jnp.zeros((bins, lane), jnp.float32)
            if layer < STEPS:
                cells[STEPS - layer] = jnp.zeros(cells.shape[1:], jnp.float32)

    @pl.when(called)
    def _():
        pl.semaphore_wait(call_sem, 1)

        @pl.when(p == 0)
        def _():
            remote_row(0, 0, 0, 0).start()

    def arrived(layer):
        @pl.when(is_row(layer))
        def _():
            there = n0.at[STEPS - layer, body]
            pltpu.make_async_copy(there, there, row_recv.at[layer]).wait()

    def cell_arrived(layer):
        @pl.when(is_row(layer))
        def _():
            there = cells.at[STEPS - layer]
            pltpu.make_async_copy(there, there, cell_recv.at[layer]).wait()

    def to_mate(layer):
        return pltpu.make_async_remote_copy(
            n0.at[STEPS - layer, body], n0.at[STEPS + 1 + layer, body],
            mate_send.at[layer], mate_recv.at[layer], device_id=mate_id, device_id_type=MESH,
        )

    def cell_to_mate(layer):
        return pltpu.make_async_remote_copy(
            cells.at[STEPS - layer], cells.at[STEPS + 1 + layer],
            mate_cell_send.at[layer], mate_cell_recv.at[layer],
            device_id=mate_id, device_id_type=MESH,
        )

    gifts = [to_mate(layer) for layer in range(STEPS)]
    cell_gifts = [cell_to_mate(layer) for layer in range(STEPS - 1)]
    offset = lax.broadcasted_iota(jnp.int32, (CHUNK, lane), 0).astype(jnp.float32)
    first_size = 0.5 + 0.5 * (offset + 0.5) / bins

    def weigh(place):
        row = row_at(place)
        mine_0, mine_1 = cells[place, 0:1], cells[place, 1:2]
        down = cells[place, 4:5] == 0.0
        below = jnp.where(down, mine_0, 0.0) * jnp.where(row > 0, 1.0, 0.0)
        above = jnp.where(down, 0.0, mine_0) * jnp.where(row < last, 1.0, 0.0)
        core = jnp.where(p == 0, 1.0, 0.0)
        return (
            mine_0 + mine_1, mine_1, core * below + (1.0 - core) * above,
            core * above + (1.0 - core) * below, cells[place, 2:3], cells[place, 3:4],
            jnp.broadcast_to(cells[place, 5:6].astype(jnp.int32), (CHUNK, lane)),
        )

    def births(source, at):
        high, low = split(source[at, PAD:])
        both = jnp.dot(
            table[...], jnp.concatenate([high, low], axis=1), preferred_element_type=jnp.float32
        )
        rest = jnp.dot(table_low[...], high, preferred_element_type=jnp.float32)
        return both[:, :lane] + both[:, lane:] + rest

    def advance(source, goal, at, weights, birth):
        total, side, before, after, grow, fragment, lookup = weights
        for i in range(bins // CHUNK):
            low, high = i * CHUNK, (i + 1) * CHUNK
            n = source[at, PAD + low : PAD + high]
            lower = source[at, PAD - 1 + low : PAD - 1 + high]
            previous = source[at - 1, PAD + low : PAD + high]
            following = source[at + 1, PAD + low : PAD + high]
            lateral = jnp.take_along_axis(n, lookup, axis=1, mode="promise_in_bounds")
            size = first_size + 0.5 * low / bins
            moved = total * n - side * lateral - before * previous - after * following
            goal[at - 1, PAD + low : PAD + high] = (
                n - size * moved - grow * (n - lower) + fragment * birth[low:high]
            )

    arrived(0)
    gifts[0].start()
    for layer in range(STEPS):
        cell_arrived(layer)
        if layer < STEPS - 1:
            cell_gifts[layer].start()
    arrived(1)
    gifts[1].start()
    weights = {place: weigh(place) for place in (3, 2, 1)}
    birth_3, birth_2 = births(n0, 3), births(n0, 2)
    gifts[0].wait_recv()
    advance(n0, n1, 3, weights[3], birth_3)
    birth_4 = births(n0, 4)
    arrived(2)
    gifts[2].start()
    advance(n0, n1, 2, weights[2], birth_2)
    for gift in cell_gifts:
        gift.wait_recv()
    weights.update({place: weigh(place) for place in (4, 5)})
    birth_1 = births(n0, 1)
    gifts[1].wait_recv()
    advance(n0, n1, 4, weights[4], birth_4)
    birth_5 = births(n0, 5)
    advance(n1, n2, 2, weights[3], births(n1, 2))
    arrived(3)
    advance(n0, n1, 1, weights[1], birth_1)
    advance(n1, n2, 1, weights[2], births(n1, 1))
    gifts[2].wait_recv()
    advance(n0, n1, 5, weights[5], birth_5)
    advance(n1, n2, 3, weights[4], births(n1, 3))
    advance(n2, n3, 1, weights[3], births(n2, 1))

    slot = 2 * k + p
    upper = slot >= rows
    holder = 2 * m + jnp.where(upper, 1, 0)
    slot = jnp.where(upper, slot - rows, slot)
    holds = holder == c

    def part(j):
        return n3.at[0, pl.ds(pl.multiple_of(PAD + local_bins * j, PAD), local_bins)]

    def remote_back(j):
        return pltpu.make_async_remote_copy(
            part(j), back.at[slot], back_send.at[j], back_recv,
            device_id=(holder, j), device_id_type=MESH,
        )

    @pl.loop(1, group)
    def _(i):
        j = k + i
        remote_back(jnp.where(j >= group, j - group, j)).start()

    @pl.when(holds)
    def _():
        pltpu.make_async_copy(part(k), back.at[slot], back_recv).start()

    @pl.when(jnp.logical_not(holds))
    def _():
        remote_back(k).start()

    for gift in gifts + cell_gifts:
        gift.wait_send()

    @pl.when(beside)
    def _():
        for q, layer in far:
            remote_row(q, layer, far_cell, k).wait_send()

    for layer in range(STEPS + 1):
        if layer < STEPS:
            core, chip = target(k, layer)
            go, _ = cases(core, chip)
            outside = jnp.logical_or(chip < 0, chip >= group)

            @pl.when(jnp.logical_or(go, jnp.logical_and(outside, beside)))
            def _():
                remote_cell(layer, far_cell, k).wait_send()

        @pl.loop(0, rows)
        def _(q):
            core, chip = target(q, layer)
            go, _ = cases(core, chip)

            @pl.when(go)
            def _():
                remote_row(q, layer, far_cell, k).wait_send()

    pltpu.make_async_copy(back, back, back_recv).wait()
    for q in range(rows):
        out[pl.ds(q, local_bins, stride=rows), :] = back[q]

    @pl.loop(1, group)
    def _(i):
        j = k + i
        remote_back(jnp.where(j >= group, j - group, j)).wait_send()

    @pl.when(jnp.logical_not(holds))
    def _():
        remote_back(k).wait_send()


def on_device(pairs, group, density, velocity, growth, rate, yields, direction, neighbour):
    local_bins, rows, lane = density.shape
    bins = yields.shape[0]
    f32, dma = jnp.float32, pltpu.SemaphoreType.DMA
    padded = PAD + bins
    result = pl.pallas_call(
        functools.partial(kernel, pairs, group, rows, local_bins, bins),
        out_shape=pltpu.VMEM((local_bins * rows, lane), f32),
        in_specs=[pl.BlockSpec(memory_space=pltpu.HBM)] * 7,
        out_specs=pl.BlockSpec(memory_space=pltpu.VMEM),
        scratch_shapes=[
            pltpu.VMEM((local_bins * rows, lane), f32),
            pltpu.VMEM((2, 1, lane), f32),
            pltpu.VMEM((2, rows, lane), f32),
            pltpu.VMEM((2, rows, lane), jnp.int32),
            pltpu.VMEM((1, bins), f32),
            pltpu.VMEM((rows, local_bins, lane), f32),
            pltpu.VMEM((8, lane), f32),
            pltpu.VMEM((rows, local_bins, lane), f32),
            pltpu.VMEM((2 * STEPS + 1, padded, lane), f32),
            pltpu.VMEM((2 * STEPS - 1, padded, lane), f32),
            pltpu.VMEM((2 * STEPS - 3, padded, lane), f32),
            pltpu.VMEM((1, padded, lane), f32),
            pltpu.VMEM((2 * STEPS, 8, lane), f32),
            pltpu.VMEM((bins, bins), jnp.bfloat16),
            pltpu.VMEM((bins, bins), jnp.bfloat16),
            dma((7,)),
            dma((STEPS,)),
            dma((STEPS,)),
            dma((4 * rows,)),
            dma((STEPS + 1,)),
            dma((STEPS,)),
            dma((STEPS,)),
            dma((group,)),
            dma,
            dma((STEPS - 1,)),
            dma((STEPS - 1,)),
            pltpu.SemaphoreType.REGULAR,
        ],
        compiler_params=pltpu.CompilerParams(
            collective_id=0, has_side_effects=True, vmem_limit_bytes=60 * 2**20
        ),
        cost_estimate=pl.CostEstimate(flops=10**9, bytes_accessed=2**21, transcendentals=0),
    )(
        density.reshape(local_bins * rows, lane), velocity, growth, rate, yields.reshape(1, bins),
        direction, neighbour,
    )
    return result.reshape(density.shape)


def solution(mesh):
    return jax.shard_map(
        functools.partial(on_device, mesh.shape["cell"] // 2, mesh.shape["bin"]),
        mesh=mesh,
        in_specs=(
            P("bin", "cell", None),
            P(None, ("cell", "bin"), None),
            P("cell", None),
            P("cell", None),
            P(),
            P("cell", None),
            P("cell", None),
        ),
        out_specs=P("bin", "cell", None),
        check_vma=False,
    )
```

```python
import functools

import jax
import jax.numpy as jnp
from jax import lax
from jax.experimental import pallas as pl
from jax.experimental.pallas import tpu as pltpu
from jax.sharding import PartitionSpec as P

MESH = pl.DeviceIdType.MESH
STEPS = 3
PAD = 8
CHUNK = 64


def split(value):
    high = value.astype(jnp.bfloat16)
    low = (value - high.astype(jnp.float32)).astype(jnp.bfloat16)
    return high, low


def kernel(
    pairs, group, rows, local_bins, bins,
    density, velocity, growth, rate, yields, direction, neighbour,
    out,
    dense, speed, cells_f, cells_i, yield_row,
    sent_rows, sent_cells, back, n0, n1, n2, n3, cells, table, table_low,
    load_sem, cell_send, cell_recv, row_send, row_recv, mate_send, mate_recv, back_send, back_recv,
    mate_cell_send, mate_cell_recv, call_sem,
):
    c, k = lax.axis_index("cell"), lax.axis_index("bin")
    m, p = c // 2, c % 2

    barrier = pltpu.get_barrier_semaphore()
    slow_pair = m == 0
    slow = jnp.logical_and(c == 0, k == 0)
    called = jnp.logical_and(
        jnp.logical_and(slow_pair, jnp.logical_not(slow)), jnp.logical_or(p == 0, 2 * k < group)
    )
    beside = jnp.logical_or(
        jnp.logical_and(p == 0, m > 0), jnp.logical_and(p == 1, m < pairs - 1)
    )
    on_edge = jnp.logical_or(
        jnp.logical_and(p == 0, k < 2), jnp.logical_and(p == 1, k >= group - 2)
    )

    def greet(cell, bin_at):
        pl.semaphore_signal(barrier, inc=1, device_id=(cell, bin_at), device_id_type=MESH)

    y, x = lax.div(k, 2), lax.rem(k, 2)
    ring = group // 2

    def chip_at(up, flip):
        along = y + up
        along = jnp.where(along >= ring, along - ring, along)
        return 2 * along + (1 - x if flip else x)

    others = [
        chip_at(up, flip)
        for up, flip in sorted(
            ((up, flip) for up in range(ring) for flip in (0, 1) if up or flip),
            key=lambda at: (-min(at[0], ring - at[0]) - at[1], -at[1]),
        )
    ]
    @pl.when(jnp.logical_and(beside, on_edge))
    def _():
        for j in range(group):
            greet(jnp.where(p == 0, c - 1, c + 1), j)

    @pl.when(jnp.logical_not(slow))
    def _():
        for bin_at in others:
            for core in (0, 1):
                greet(2 * m + core, bin_at)
        greet(2 * m + 1 - p, k)

    loads = [
        pltpu.make_async_copy(density, dense, load_sem.at[0]),
        pltpu.make_async_copy(velocity, speed, load_sem.at[1]),
        pltpu.make_async_copy(growth, cells_f.at[0], load_sem.at[2]),
        pltpu.make_async_copy(rate, cells_f.at[1], load_sem.at[3]),
        pltpu.make_async_copy(direction, cells_i.at[0], load_sem.at[4]),
        pltpu.make_async_copy(neighbour, cells_i.at[1], load_sem.at[5]),
        pltpu.make_async_copy(yields, yield_row, load_sem.at[6]),
    ]
    for load in loads:
        load.start()

    @pl.when(slow)
    def _():
        pl.semaphore_wait(barrier, 2 * group - 1)
        for i in range(1, group + group // 2):
            pl.semaphore_signal(
                call_sem, inc=1, device_id=(i // group, i % group), device_id_type=MESH
            )

    for load in loads:
        load.wait()

    for q in range(rows):
        sent_rows[q] = dense[pl.ds(q, local_bins, stride=rows), :]
    sent_cells[0:1] = speed[0]
    sent_cells[1:2] = speed[1]
    sent_cells[2:3] = cells_f[0, pl.ds(k, 1), :]
    sent_cells[3:4] = cells_f[1, pl.ds(k, 1), :]
    sent_cells[4:5] = cells_i[0, pl.ds(k, 1), :].astype(jnp.float32)
    sent_cells[5:6] = cells_i[1, pl.ds(k, 1), :].astype(jnp.float32)
    sent_cells[6:8] = jnp.zeros((2, sent_cells.shape[1]), jnp.float32)

    @pl.when(jnp.logical_not(slow))
    def _():
        pl.semaphore_wait(
            barrier, 2 * group - 1 + jnp.where(beside, 2, 0) - jnp.where(slow_pair, 1, 0)
        )

    mine = pl.ds(pl.multiple_of(PAD + local_bins * k, PAD), local_bins)
    first_chip = p * (rows // 2)

    def target(q, layer):
        half = lax.div(q, 2)
        odd = q - 2 * half
        shift = (layer + 1) // 2
        core = odd if layer % 2 == 0 else 1 - odd
        return core, first_chip + half + shift - 2 * shift * core

    def cases(core, chip):
        near = jnp.logical_and(chip >= 0, chip < group)
        here = jnp.logical_and(chip == k, core == p)
        return jnp.logical_and(near, jnp.logical_not(here)), here

    def remote_row(q, layer, cell, bin_at):
        return pltpu.make_async_remote_copy(
            sent_rows.at[q], n0.at[STEPS - layer, mine], row_send.at[layer * rows + q],
            row_recv.at[layer], device_id=(cell, bin_at), device_id_type=MESH,
        )

    def remote_cell(layer, cell, bin_at):
        return pltpu.make_async_remote_copy(
            sent_cells, cells.at[STEPS - layer], cell_send.at[layer], cell_recv.at[layer],
            device_id=(cell, bin_at), device_id_type=MESH,
        )

    far_cell = jnp.where(p == 0, c - 1, c + 1)
    far_first = jnp.where(p == 0, group, -group)
    far = []
    for u, layer in ((0, 1), (1, 2), (2, 3), (0, 3)):
        far.append((jnp.where(p == 0, u, rows - 1 - u), layer))

    @pl.when(beside)
    def _():
        for q, layer in far:
            _, chip = target(q, layer)
            remote_row(q, layer, far_cell, chip + far_first).start()

    called_0 = jnp.logical_and(called, p == 0)

    def send_rows(layer):
        for chip in others:
            for core in (0, 1):
                q = 2 * (chip - first_chip) + (1 + layer if core else -layer)
                go = jnp.logical_and(q >= 0, q < rows)
                if core == 0:
                    early = jnp.logical_and(layer == 0, chip == 0)
                    go = jnp.logical_and(go, jnp.logical_not(jnp.logical_and(called_0, early)))

                @pl.when(go)
                def _():
                    remote_row(q, layer, 2 * m + core, chip).start()

        for core in (0, 1):
            q = 2 * (k - first_chip) + (1 + layer if core else -layer)
            go = jnp.logical_and(q >= 0, q < rows)

            @pl.when(jnp.logical_and(go, p != core))
            def _():
                remote_row(q, layer, 2 * m + core, k).start()

            @pl.when(jnp.logical_and(go, p == core))
            def _():
                pltpu.make_async_copy(
                    sent_rows.at[q], n0.at[STEPS - layer, mine], row_recv.at[layer]
                ).start()

    send_rows(0)
    for layer in range(STEPS):
        core, chip = target(k, layer)
        go, here = cases(core, chip)
        outside = jnp.logical_or(chip < 0, chip >= group)

        @pl.when(go)
        def _():
            remote_cell(layer, 2 * m + core, chip).start()

        @pl.when(here)
        def _():
            pltpu.make_async_copy(
                sent_cells, cells.at[STEPS - layer], cell_recv.at[layer]
            ).start()

        @pl.when(jnp.logical_and(outside, beside))
        def _():
            remote_cell(layer, far_cell, chip + far_first).start()

    @pl.loop(1, STEPS + 1)
    def _(layer):
        send_rows(layer)

    spread = jnp.broadcast_to(yield_row[...], (bins, bins))
    spread = pltpu.roll(spread, 0, 1, stride=1, stride_axis=0)
    at_b = lax.broadcasted_iota(jnp.int32, (bins, bins), 0)
    at_a = lax.broadcasted_iota(jnp.int32, (bins, bins), 1)
    high, low = split(jnp.where(at_a >= at_b, spread, 0.0))
    table[...] = high
    table_low[...] = low

    lane = n0.shape[-1]
    zero = jnp.zeros((PAD, lane), jnp.float32)
    for buffer in (n0, n1, n2, n3):
        for place in range(buffer.shape[0]):
            buffer[place, 0:PAD] = zero

    body = pl.ds(PAD, bins)
    mate_id = (2 * m + 1 - p, k)
    first = 2 * (m * group + k)
    last = 2 * pairs * rows - 1

    def row_at(place):
        return first + jnp.where(p == 0, place - STEPS, STEPS + 1 - place)

    def is_row(layer):
        row = row_at(STEPS - layer)
        return jnp.logical_and(row >= 0, row <= last)

    for layer in range(1, STEPS + 1):
        @pl.when(jnp.logical_not(is_row(layer)))
        def _():
            n0[STEPS - layer, PAD:] = jnp.zeros((bins, lane), jnp.float32)
            if layer < STEPS:
                cells[STEPS - layer] = jnp.zeros(cells.shape[1:], jnp.float32)

    @pl.when(called)
    def _():
        pl.semaphore_wait(call_sem, 1)

        @pl.when(p == 0)
        def _():
            remote_row(0, 0, 0, 0).start()

    def arrived(layer):
        @pl.when(is_row(layer))
        def _():
            there = n0.at[STEPS - layer, body]
            pltpu.make_async_copy(there, there, row_recv.at[layer]).wait()

    def cell_arrived(layer):
        @pl.when(is_row(layer))
        def _():
            there = cells.at[STEPS - layer]
            pltpu.make_async_copy(there, there, cell_recv.at[layer]).wait()

    def to_mate(layer):
        return pltpu.make_async_remote_copy(
            n0.at[STEPS - layer, body], n0.at[STEPS + 1 + layer, body],
            mate_send.at[layer], mate_recv.at[layer], device_id=mate_id, device_id_type=MESH,
        )

    def cell_to_mate(layer):
        return pltpu.make_async_remote_copy(
            cells.at[STEPS - layer], cells.at[STEPS + 1 + layer],
            mate_cell_send.at[layer], mate_cell_recv.at[layer],
            device_id=mate_id, device_id_type=MESH,
        )

    gifts = [to_mate(layer) for layer in range(STEPS)]
    cell_gifts = [cell_to_mate(layer) for layer in range(STEPS - 1)]
    offset = lax.broadcasted_iota(jnp.int32, (CHUNK, lane), 0).astype(jnp.float32)
    first_size = 0.5 + 0.5 * (offset + 0.5) / bins

    def weigh(place):
        row = row_at(place)
        mine_0, mine_1 = cells[place, 0:1], cells[place, 1:2]
        down = cells[place, 4:5] == 0.0
        below = jnp.where(down, mine_0, 0.0) * jnp.where(row > 0, 1.0, 0.0)
        above = jnp.where(down, 0.0, mine_0) * jnp.where(row < last, 1.0, 0.0)
        core = jnp.where(p == 0, 1.0, 0.0)
        return (
            mine_0 + mine_1, mine_1, core * below + (1.0 - core) * above,
            core * above + (1.0 - core) * below, cells[place, 2:3], cells[place, 3:4],
            jnp.broadcast_to(cells[place, 5:6].astype(jnp.int32), (CHUNK, lane)),
        )

    def births(source, at):
        high, low = split(source[at, PAD:])
        both = jnp.dot(
            table[...], jnp.concatenate([high, low], axis=1), preferred_element_type=jnp.float32
        )
        rest = jnp.dot(table_low[...], high, preferred_element_type=jnp.float32)
        return both[:, :lane] + both[:, lane:] + rest

    def advance(source, goal, at, weights, birth, with_before=True, with_after=True):
        total, side, before, after, grow, fragment, lookup = weights
        for i in range(bins // CHUNK):
            low, high = i * CHUNK, (i + 1) * CHUNK
            n = source[at, PAD + low : PAD + high]
            lower = source[at, PAD - 1 + low : PAD - 1 + high]
            lateral = jnp.take_along_axis(n, lookup, axis=1, mode="promise_in_bounds")
            size = first_size + 0.5 * low / bins
            moved = total * n - side * lateral
            if with_before:
                moved -= before * source[at - 1, PAD + low : PAD + high]
            if with_after:
                moved -= after * source[at + 1, PAD + low : PAD + high]
            goal[at - 1, PAD + low : PAD + high] = (
                n - size * moved - grow * (n - lower) + fragment * birth[low:high]
            )

    arrived(0)
    gifts[0].start()
    for layer in range(STEPS):
        cell_arrived(layer)
        if layer < STEPS - 1:
            cell_gifts[layer].start()
    arrived(1)
    gifts[1].start()
    weights = {place: weigh(place) for place in (3, 2, 1)}
    birth_3, birth_2 = births(n0, 3), births(n0, 2)
    gifts[0].wait_recv()
    advance(n0, n1, 3, weights[3], birth_3)
    birth_4 = births(n0, 4)
    arrived(2)
    gifts[2].start()
    advance(n0, n1, 2, weights[2], birth_2)
    advance(n0, n1, 1, weights[1], births(n0, 1), with_before=False)
    for gift in cell_gifts:
        gift.wait_recv()
    weights.update({place: weigh(place) for place in (4, 5)})
    gifts[1].wait_recv()
    advance(n0, n1, 4, weights[4], birth_4)
    advance(n0, n1, 5, weights[5], births(n0, 5), with_after=False)
    advance(n1, n2, 2, weights[3], births(n1, 2))
    advance(n1, n2, 1, weights[2], births(n1, 1), with_before=False)
    advance(n1, n2, 3, weights[4], births(n1, 3), with_after=False)
    advance(n2, n3, 1, weights[3], births(n2, 1), with_before=False, with_after=False)

    arrived(3)
    gifts[2].wait_recv()
    for i in range(bins // CHUNK):
        low, high = i * CHUNK, (i + 1) * CHUNK
        here = pl.ds(PAD + low, CHUNK)
        size = first_size + 0.5 * low / bins
        one = n1[0, here] + size * (weights[1][2] * n0[0, here])
        two = n2[0, here] + size * (weights[2][2] * one)
        other_one = n1[4, here] + size * (weights[5][3] * n0[6, here])
        other_two = n2[2, here] + size * (weights[4][3] * other_one)
        n3[0, here] += size * (weights[3][2] * two + weights[3][3] * other_two)

    slot = 2 * k + p
    upper = slot >= rows
    holder = 2 * m + jnp.where(upper, 1, 0)
    slot = jnp.where(upper, slot - rows, slot)
    holds = holder == c

    def part(j):
        return n3.at[0, pl.ds(pl.multiple_of(PAD + local_bins * j, PAD), local_bins)]

    def remote_back(j):
        return pltpu.make_async_remote_copy(
            part(j), back.at[slot], back_send.at[j], back_recv,
            device_id=(holder, j), device_id_type=MESH,
        )

    for j in others:
        remote_back(j).start()

    @pl.when(holds)
    def _():
        pltpu.make_async_copy(part(k), back.at[slot], back_recv).start()

    @pl.when(jnp.logical_not(holds))
    def _():
        remote_back(k).start()

    for gift in gifts + cell_gifts:
        gift.wait_send()

    @pl.when(beside)
    def _():
        for q, layer in far:
            remote_row(q, layer, far_cell, k).wait_send()

    for layer in range(STEPS + 1):
        if layer < STEPS:
            core, chip = target(k, layer)
            go, _ = cases(core, chip)
            outside = jnp.logical_or(chip < 0, chip >= group)

            @pl.when(jnp.logical_or(go, jnp.logical_and(outside, beside)))
            def _():
                remote_cell(layer, far_cell, k).wait_send()

        @pl.loop(0, rows)
        def _(q):
            core, chip = target(q, layer)
            go, _ = cases(core, chip)

            @pl.when(go)
            def _():
                remote_row(q, layer, far_cell, k).wait_send()

    pltpu.make_async_copy(back, back, back_recv).wait()
    for q in range(rows):
        out[pl.ds(q, local_bins, stride=rows), :] = back[q]

    for j in others:
        remote_back(j).wait_send()

    @pl.when(jnp.logical_not(holds))
    def _():
        remote_back(k).wait_send()


def on_device(pairs, group, density, velocity, growth, rate, yields, direction, neighbour):
    local_bins, rows, lane = density.shape
    bins = yields.shape[0]
    f32, dma = jnp.float32, pltpu.SemaphoreType.DMA
    padded = PAD + bins
    result = pl.pallas_call(
        functools.partial(kernel, pairs, group, rows, local_bins, bins),
        out_shape=pltpu.VMEM((local_bins * rows, lane), f32),
        in_specs=[pl.BlockSpec(memory_space=pltpu.HBM)] * 7,
        out_specs=pl.BlockSpec(memory_space=pltpu.VMEM),
        scratch_shapes=[
            pltpu.VMEM((local_bins * rows, lane), f32),
            pltpu.VMEM((2, 1, lane), f32),
            pltpu.VMEM((2, rows, lane), f32),
            pltpu.VMEM((2, rows, lane), jnp.int32),
            pltpu.VMEM((1, bins), f32),
            pltpu.VMEM((rows, local_bins, lane), f32),
            pltpu.VMEM((8, lane), f32),
            pltpu.VMEM((rows, local_bins, lane), f32),
            pltpu.VMEM((2 * STEPS + 1, padded, lane), f32),
            pltpu.VMEM((2 * STEPS - 1, padded, lane), f32),
            pltpu.VMEM((2 * STEPS - 3, padded, lane), f32),
            pltpu.VMEM((1, padded, lane), f32),
            pltpu.VMEM((2 * STEPS, 8, lane), f32),
            pltpu.VMEM((bins, bins), jnp.bfloat16),
            pltpu.VMEM((bins, bins), jnp.bfloat16),
            dma((7,)),
            dma((STEPS,)),
            dma((STEPS,)),
            dma((4 * rows,)),
            dma((STEPS + 1,)),
            dma((STEPS,)),
            dma((STEPS,)),
            dma((group,)),
            dma,
            dma((STEPS - 1,)),
            dma((STEPS - 1,)),
            pltpu.SemaphoreType.REGULAR,
        ],
        compiler_params=pltpu.CompilerParams(
            collective_id=0, has_side_effects=True, vmem_limit_bytes=60 * 2**20
        ),
        cost_estimate=pl.CostEstimate(flops=10**9, bytes_accessed=2**21, transcendentals=0),
    )(
        density.reshape(local_bins * rows, lane), velocity, growth, rate, yields.reshape(1, bins),
        direction, neighbour,
    )
    return result.reshape(density.shape)


def solution(mesh):
    return jax.shard_map(
        functools.partial(on_device, mesh.shape["cell"] // 2, mesh.shape["bin"]),
        mesh=mesh,
        in_specs=(
            P("bin", "cell", None),
            P(None, ("cell", "bin"), None),
            P("cell", None),
            P("cell", None),
            P(),
            P("cell", None),
            P("cell", None),
        ),
        out_specs=P("bin", "cell", None),
        check_vma=False,
    )
```

```python
import functools

import jax
import jax.numpy as jnp
from jax import lax
from jax.experimental import pallas as pl
from jax.experimental.pallas import tpu as pltpu
from jax.sharding import PartitionSpec as P

MESH = pl.DeviceIdType.MESH
STEPS = 3
PAD = 8
CHUNK = 64


def split(value):
    high = value.astype(jnp.bfloat16)
    low = (value - high.astype(jnp.float32)).astype(jnp.bfloat16)
    return high, low


def kernel(
    pairs, group, rows, local_bins, bins,
    density, velocity, growth, rate, yields, direction, neighbour,
    out,
    dense, speed, cells_f, cells_i, yield_row,
    sent_rows, sent_cells, back, n0, n1, n2, n3, cells, table, table_low,
    load_sem, cell_send, cell_recv, row_send, row_recv, mate_send, mate_recv, back_send, back_recv,
    mate_cell_send, mate_cell_recv, call_sem,
):
    c, k = lax.axis_index("cell"), lax.axis_index("bin")
    m, p = c // 2, c % 2

    barrier = pltpu.get_barrier_semaphore()
    slow_pair = m == 0
    slow = jnp.logical_and(c == 0, k == 0)
    called = jnp.logical_and(
        jnp.logical_and(slow_pair, jnp.logical_not(slow)), jnp.logical_or(p == 0, 2 * k < group)
    )
    beside = jnp.logical_or(
        jnp.logical_and(p == 0, m > 0), jnp.logical_and(p == 1, m < pairs - 1)
    )
    on_edge = jnp.logical_or(
        jnp.logical_and(p == 0, k < 2), jnp.logical_and(p == 1, k >= group - 2)
    )

    def greet(cell, bin_at):
        pl.semaphore_signal(barrier, inc=1, device_id=(cell, bin_at), device_id_type=MESH)

    y, x = lax.div(k, 2), lax.rem(k, 2)
    ring = group // 2

    def chip_at(up, flip):
        along = y + up
        along = jnp.where(along >= ring, along - ring, along)
        return 2 * along + (1 - x if flip else x)

    others = [
        chip_at(up, flip)
        for up, flip in sorted(
            ((up, flip) for up in range(ring) for flip in (0, 1) if up or flip),
            key=lambda at: (-min(at[0], ring - at[0]) - at[1], -at[1]),
        )
    ]
    @pl.when(jnp.logical_and(beside, on_edge))
    def _():
        for j in range(group):
            greet(jnp.where(p == 0, c - 1, c + 1), j)

    @pl.when(jnp.logical_not(slow))
    def _():
        for bin_at in others:
            for core in (0, 1):
                greet(2 * m + core, bin_at)
        greet(2 * m + 1 - p, k)

    loads = [
        pltpu.make_async_copy(density, dense, load_sem.at[0]),
        pltpu.make_async_copy(velocity, speed, load_sem.at[1]),
        pltpu.make_async_copy(growth, cells_f.at[0], load_sem.at[2]),
        pltpu.make_async_copy(rate, cells_f.at[1], load_sem.at[3]),
        pltpu.make_async_copy(direction, cells_i.at[0], load_sem.at[4]),
        pltpu.make_async_copy(neighbour, cells_i.at[1], load_sem.at[5]),
        pltpu.make_async_copy(yields, yield_row, load_sem.at[6]),
    ]
    for load in loads:
        load.start()

    @pl.when(slow)
    def _():
        pl.semaphore_wait(barrier, 2 * group - 1)
        for i in range(1, group + group // 2):
            pl.semaphore_signal(
                call_sem, inc=1, device_id=(i // group, i % group), device_id_type=MESH
            )

    for load in loads:
        load.wait()

    for q in range(rows):
        sent_rows[q] = dense[pl.ds(q, local_bins, stride=rows), :]
    sent_cells[0:1] = speed[0]
    sent_cells[1:2] = speed[1]
    sent_cells[2:3] = cells_f[0, pl.ds(k, 1), :]
    sent_cells[3:4] = cells_f[1, pl.ds(k, 1), :]
    sent_cells[4:5] = cells_i[0, pl.ds(k, 1), :].astype(jnp.float32)
    sent_cells[5:6] = cells_i[1, pl.ds(k, 1), :].astype(jnp.float32)
    sent_cells[6:8] = jnp.zeros((2, sent_cells.shape[1]), jnp.float32)

    @pl.when(jnp.logical_not(slow))
    def _():
        pl.semaphore_wait(
            barrier, 2 * group - 1 + jnp.where(beside, 2, 0) - jnp.where(slow_pair, 1, 0)
        )

    mine = pl.ds(pl.multiple_of(PAD + local_bins * k, PAD), local_bins)
    first_chip = p * (rows // 2)

    def target(q, layer):
        half = lax.div(q, 2)
        odd = q - 2 * half
        shift = (layer + 1) // 2
        core = odd if layer % 2 == 0 else 1 - odd
        return core, first_chip + half + shift - 2 * shift * core

    def cases(core, chip):
        near = jnp.logical_and(chip >= 0, chip < group)
        here = jnp.logical_and(chip == k, core == p)
        return jnp.logical_and(near, jnp.logical_not(here)), here

    def remote_row(q, layer, cell, bin_at):
        return pltpu.make_async_remote_copy(
            sent_rows.at[q], n0.at[STEPS - layer, mine], row_send.at[layer * rows + q],
            row_recv.at[layer], device_id=(cell, bin_at), device_id_type=MESH,
        )

    def remote_cell(layer, cell, bin_at):
        return pltpu.make_async_remote_copy(
            sent_cells, cells.at[STEPS - layer], cell_send.at[layer], cell_recv.at[layer],
            device_id=(cell, bin_at), device_id_type=MESH,
        )

    far_cell = jnp.where(p == 0, c - 1, c + 1)
    far_first = jnp.where(p == 0, group, -group)
    far = []
    for u, layer in ((0, 1), (1, 2), (2, 3), (0, 3)):
        far.append((jnp.where(p == 0, u, rows - 1 - u), layer))

    @pl.when(beside)
    def _():
        for q, layer in far:
            _, chip = target(q, layer)
            remote_row(q, layer, far_cell, chip + far_first).start()

    called_0 = jnp.logical_and(called, p == 0)

    def send_rows(layer):
        for chip in others:
            for core in (0, 1):
                q = 2 * (chip - first_chip) + (1 + layer if core else -layer)
                go = jnp.logical_and(q >= 0, q < rows)
                if core == 0:
                    early = jnp.logical_and(layer == 0, chip == 0)
                    go = jnp.logical_and(go, jnp.logical_not(jnp.logical_and(called_0, early)))

                @pl.when(go)
                def _():
                    remote_row(q, layer, 2 * m + core, chip).start()

        for core in (0, 1):
            q = 2 * (k - first_chip) + (1 + layer if core else -layer)
            go = jnp.logical_and(q >= 0, q < rows)

            @pl.when(jnp.logical_and(go, p != core))
            def _():
                remote_row(q, layer, 2 * m + core, k).start()

            @pl.when(jnp.logical_and(go, p == core))
            def _():
                pltpu.make_async_copy(
                    sent_rows.at[q], n0.at[STEPS - layer, mine], row_recv.at[layer]
                ).start()

    send_rows(0)
    for layer in range(STEPS):
        core, chip = target(k, layer)
        go, here = cases(core, chip)
        outside = jnp.logical_or(chip < 0, chip >= group)

        @pl.when(go)
        def _():
            remote_cell(layer, 2 * m + core, chip).start()

        @pl.when(here)
        def _():
            pltpu.make_async_copy(
                sent_cells, cells.at[STEPS - layer], cell_recv.at[layer]
            ).start()

        @pl.when(jnp.logical_and(outside, beside))
        def _():
            remote_cell(layer, far_cell, chip + far_first).start()

    @pl.loop(1, STEPS + 1)
    def _(layer):
        send_rows(layer)

    spread = jnp.broadcast_to(yield_row[...], (bins, bins))
    spread = pltpu.roll(spread, 0, 1, stride=1, stride_axis=0)
    at_b = lax.broadcasted_iota(jnp.int32, (bins, bins), 0)
    at_a = lax.broadcasted_iota(jnp.int32, (bins, bins), 1)
    high, low = split(jnp.where(at_a >= at_b, spread, 0.0))
    table[...] = high
    table_low[...] = low

    lane = n0.shape[-1]
    zero = jnp.zeros((PAD, lane), jnp.float32)
    for buffer in (n0, n1, n2, n3):
        for place in range(buffer.shape[0]):
            buffer[place, 0:PAD] = zero

    body = pl.ds(PAD, bins)
    mate_id = (2 * m + 1 - p, k)
    first = 2 * (m * group + k)
    last = 2 * pairs * rows - 1

    def row_at(place):
        return first + jnp.where(p == 0, place - STEPS, STEPS + 1 - place)

    def is_row(layer):
        row = row_at(STEPS - layer)
        return jnp.logical_and(row >= 0, row <= last)

    for layer in range(1, STEPS + 1):
        @pl.when(jnp.logical_not(is_row(layer)))
        def _():
            n0[STEPS - layer, PAD:] = jnp.zeros((bins, lane), jnp.float32)
            if layer < STEPS:
                cells[STEPS - layer] = jnp.zeros(cells.shape[1:], jnp.float32)

    @pl.when(called)
    def _():
        pl.semaphore_wait(call_sem, 1)

        @pl.when(p == 0)
        def _():
            remote_row(0, 0, 0, 0).start()

    def arrived(layer):
        @pl.when(is_row(layer))
        def _():
            there = n0.at[STEPS - layer, body]
            pltpu.make_async_copy(there, there, row_recv.at[layer]).wait()

    def cell_arrived(layer):
        @pl.when(is_row(layer))
        def _():
            there = cells.at[STEPS - layer]
            pltpu.make_async_copy(there, there, cell_recv.at[layer]).wait()

    def to_mate(layer):
        return pltpu.make_async_remote_copy(
            n0.at[STEPS - layer, body], n0.at[STEPS + 1 + layer, body],
            mate_send.at[layer], mate_recv.at[layer], device_id=mate_id, device_id_type=MESH,
        )

    def cell_to_mate(layer):
        return pltpu.make_async_remote_copy(
            cells.at[STEPS - layer], cells.at[STEPS + 1 + layer],
            mate_cell_send.at[layer], mate_cell_recv.at[layer],
            device_id=mate_id, device_id_type=MESH,
        )

    gifts = [to_mate(layer) for layer in range(STEPS)]
    cell_gifts = [cell_to_mate(layer) for layer in range(STEPS - 1)]
    offset = lax.broadcasted_iota(jnp.int32, (CHUNK, lane), 0).astype(jnp.float32)
    first_size = 0.5 + 0.5 * (offset + 0.5) / bins

    def weigh(place):
        row = row_at(place)
        mine_0, mine_1 = cells[place, 0:1], cells[place, 1:2]
        down = cells[place, 4:5] == 0.0
        below = jnp.where(down, mine_0, 0.0) * jnp.where(row > 0, 1.0, 0.0)
        above = jnp.where(down, 0.0, mine_0) * jnp.where(row < last, 1.0, 0.0)
        core = jnp.where(p == 0, 1.0, 0.0)
        return (
            mine_0 + mine_1, mine_1, core * below + (1.0 - core) * above,
            core * above + (1.0 - core) * below, cells[place, 2:3], cells[place, 3:4],
            jnp.broadcast_to(cells[place, 5:6].astype(jnp.int32), (CHUNK, lane)),
        )

    def births(source, at):
        high, low = split(source[at, PAD:])
        both = jnp.dot(
            table[...], jnp.concatenate([high, low], axis=1), preferred_element_type=jnp.float32
        )
        rest = jnp.dot(table_low[...], high, preferred_element_type=jnp.float32)
        return both[:, :lane] + both[:, lane:] + rest

    def advance(source, goal, at, weights, birth, with_before=True, with_after=True):
        total, side, before, after, grow, fragment, lookup = weights
        for i in range(bins // CHUNK):
            low, high = i * CHUNK, (i + 1) * CHUNK
            n = source[at, PAD + low : PAD + high]
            lower = source[at, PAD - 1 + low : PAD - 1 + high]
            lateral = jnp.take_along_axis(n, lookup, axis=1, mode="promise_in_bounds")
            size = first_size + 0.5 * low / bins
            moved = total * n - side * lateral
            if with_before:
                moved -= before * source[at - 1, PAD + low : PAD + high]
            if with_after:
                moved -= after * source[at + 1, PAD + low : PAD + high]
            goal[at - 1, PAD + low : PAD + high] = (
                n - size * moved - grow * (n - lower) + fragment * birth[low:high]
            )

    arrived(0)
    gifts[0].start()
    for layer in range(STEPS):
        cell_arrived(layer)
        if layer < STEPS - 1:
            cell_gifts[layer].start()
    arrived(1)
    gifts[1].start()
    weights = {place: weigh(place) for place in (3, 2, 1)}
    birth_3, birth_2 = births(n0, 3), births(n0, 2)
    gifts[0].wait_recv()
    advance(n0, n1, 3, weights[3], birth_3)
    birth_4 = births(n0, 4)
    arrived(2)
    gifts[2].start()
    advance(n0, n1, 2, weights[2], birth_2)
    advance(n0, n1, 1, weights[1], births(n0, 1), with_before=False)
    for gift in cell_gifts:
        gift.wait_recv()
    weights.update({place: weigh(place) for place in (4, 5)})
    gifts[1].wait_recv()
    advance(n0, n1, 4, weights[4], birth_4)
    advance(n0, n1, 5, weights[5], births(n0, 5), with_after=False)
    advance(n1, n2, 2, weights[3], births(n1, 2))
    advance(n1, n2, 1, weights[2], births(n1, 1), with_before=False)
    advance(n1, n2, 3, weights[4], births(n1, 3), with_after=False)
    advance(n2, n3, 1, weights[3], births(n2, 1), with_before=False, with_after=False)

    arrived(3)
    gifts[2].wait_recv()
    for i in range(bins // CHUNK):
        low, high = i * CHUNK, (i + 1) * CHUNK
        here = pl.ds(PAD + low, CHUNK)
        size = first_size + 0.5 * low / bins
        one = n1[0, here] + size * (weights[1][2] * n0[0, here])
        two = n2[0, here] + size * (weights[2][2] * one)
        other_one = n1[4, here] + size * (weights[5][3] * n0[6, here])
        other_two = n2[2, here] + size * (weights[4][3] * other_one)
        n3[0, here] += size * (weights[3][2] * two + weights[3][3] * other_two)

    slot = 2 * k + p
    upper = slot >= rows
    holder = 2 * m + jnp.where(upper, 1, 0)
    slot = jnp.where(upper, slot - rows, slot)
    holds = holder == c

    def part(j):
        return n3.at[0, pl.ds(pl.multiple_of(PAD + local_bins * j, PAD), local_bins)]

    def remote_back(j):
        return pltpu.make_async_remote_copy(
            part(j), back.at[slot], back_send.at[j], back_recv,
            device_id=(holder, j), device_id_type=MESH,
        )

    @pl.when(holds)
    def _():
        pltpu.make_async_copy(part(k), back.at[slot], back_recv).start()

    for j in (0, 1):
        @pl.when(jnp.logical_not(jnp.logical_and(holds, k == j)))
        def _():
            remote_back(j).start()

    for j in others:
        @pl.when(j > 1)
        def _():
            remote_back(j).start()

    @pl.when(jnp.logical_and(k > 1, jnp.logical_not(holds)))
    def _():
        remote_back(k).start()

    for gift in gifts + cell_gifts:
        gift.wait_send()

    @pl.when(beside)
    def _():
        for q, layer in far:
            remote_row(q, layer, far_cell, k).wait_send()

    for layer in range(STEPS + 1):
        if layer < STEPS:
            core, chip = target(k, layer)
            go, _ = cases(core, chip)
            outside = jnp.logical_or(chip < 0, chip >= group)

            @pl.when(jnp.logical_or(go, jnp.logical_and(outside, beside)))
            def _():
                remote_cell(layer, far_cell, k).wait_send()

        @pl.loop(0, rows)
        def _(q):
            core, chip = target(q, layer)
            go, _ = cases(core, chip)

            @pl.when(go)
            def _():
                remote_row(q, layer, far_cell, k).wait_send()

    pltpu.make_async_copy(back, back, back_recv).wait()
    for q in range(rows):
        out[pl.ds(q, local_bins, stride=rows), :] = back[q]

    for j in others:
        remote_back(j).wait_send()

    @pl.when(jnp.logical_not(holds))
    def _():
        remote_back(k).wait_send()


def on_device(pairs, group, density, velocity, growth, rate, yields, direction, neighbour):
    local_bins, rows, lane = density.shape
    bins = yields.shape[0]
    f32, dma = jnp.float32, pltpu.SemaphoreType.DMA
    padded = PAD + bins
    result = pl.pallas_call(
        functools.partial(kernel, pairs, group, rows, local_bins, bins),
        out_shape=pltpu.VMEM((local_bins * rows, lane), f32),
        in_specs=[pl.BlockSpec(memory_space=pltpu.HBM)] * 7,
        out_specs=pl.BlockSpec(memory_space=pltpu.VMEM),
        scratch_shapes=[
            pltpu.VMEM((local_bins * rows, lane), f32),
            pltpu.VMEM((2, 1, lane), f32),
            pltpu.VMEM((2, rows, lane), f32),
            pltpu.VMEM((2, rows, lane), jnp.int32),
            pltpu.VMEM((1, bins), f32),
            pltpu.VMEM((rows, local_bins, lane), f32),
            pltpu.VMEM((8, lane), f32),
            pltpu.VMEM((rows, local_bins, lane), f32),
            pltpu.VMEM((2 * STEPS + 1, padded, lane), f32),
            pltpu.VMEM((2 * STEPS - 1, padded, lane), f32),
            pltpu.VMEM((2 * STEPS - 3, padded, lane), f32),
            pltpu.VMEM((1, padded, lane), f32),
            pltpu.VMEM((2 * STEPS, 8, lane), f32),
            pltpu.VMEM((bins, bins), jnp.bfloat16),
            pltpu.VMEM((bins, bins), jnp.bfloat16),
            dma((7,)),
            dma((STEPS,)),
            dma((STEPS,)),
            dma((4 * rows,)),
            dma((STEPS + 1,)),
            dma((STEPS,)),
            dma((STEPS,)),
            dma((group,)),
            dma,
            dma((STEPS - 1,)),
            dma((STEPS - 1,)),
            pltpu.SemaphoreType.REGULAR,
        ],
        compiler_params=pltpu.CompilerParams(
            collective_id=0, has_side_effects=True, vmem_limit_bytes=60 * 2**20
        ),
        cost_estimate=pl.CostEstimate(flops=10**9, bytes_accessed=2**21, transcendentals=0),
    )(
        density.reshape(local_bins * rows, lane), velocity, growth, rate, yields.reshape(1, bins),
        direction, neighbour,
    )
    return result.reshape(density.shape)


def solution(mesh):
    return jax.shard_map(
        functools.partial(on_device, mesh.shape["cell"] // 2, mesh.shape["bin"]),
        mesh=mesh,
        in_specs=(
            P("bin", "cell", None),
            P(None, ("cell", "bin"), None),
            P("cell", None),
            P("cell", None),
            P(),
            P("cell", None),
            P("cell", None),
        ),
        out_specs=P("bin", "cell", None),
        check_vma=False,
    )
```

```python
import functools

import jax
import jax.numpy as jnp
from jax import lax
from jax.experimental import pallas as pl
from jax.experimental.pallas import tpu as pltpu
from jax.sharding import PartitionSpec as P

MESH = pl.DeviceIdType.MESH
STEPS = 3
PAD = 8
CHUNK = 64


def split(value):
    high = value.astype(jnp.bfloat16)
    low = (value - high.astype(jnp.float32)).astype(jnp.bfloat16)
    return high, low


def kernel(
    pairs, group, rows, local_bins, bins,
    density, velocity, growth, rate, yields, direction, neighbour,
    out,
    dense, speed, cells_f, cells_i, yield_row,
    sent_rows, sent_cells, back, n0, n1, n2, n3, cells, table, table_low,
    load_sem, cell_send, cell_recv, row_send, row_recv, mate_send, mate_recv, back_send, back_recv,
    mate_cell_send, mate_cell_recv, call_sem,
):
    c, k = lax.axis_index("cell"), lax.axis_index("bin")
    m, p = c // 2, c % 2

    barrier = pltpu.get_barrier_semaphore()
    slow_pair = m == 0
    slow = jnp.logical_and(c == 0, k == 0)
    called = jnp.logical_and(
        jnp.logical_and(slow_pair, jnp.logical_not(slow)), jnp.logical_or(p == 0, 2 * k < group)
    )
    beside = jnp.logical_or(
        jnp.logical_and(p == 0, m > 0), jnp.logical_and(p == 1, m < pairs - 1)
    )
    on_edge = jnp.logical_or(
        jnp.logical_and(p == 0, k < 2), jnp.logical_and(p == 1, k >= group - 2)
    )

    def greet(cell, bin_at):
        pl.semaphore_signal(barrier, inc=1, device_id=(cell, bin_at), device_id_type=MESH)

    y, x = lax.div(k, 2), lax.rem(k, 2)
    ring = group // 2

    def chip_at(up, flip):
        along = y + up
        along = jnp.where(along >= ring, along - ring, along)
        return 2 * along + (1 - x if flip else x)

    others = [
        chip_at(up, flip)
        for up, flip in sorted(
            ((up, flip) for up in range(ring) for flip in (0, 1) if up or flip),
            key=lambda at: (-min(at[0], ring - at[0]) - at[1], -at[1]),
        )
    ]
    @pl.when(jnp.logical_and(beside, on_edge))
    def _():
        for j in range(group):
            greet(jnp.where(p == 0, c - 1, c + 1), j)

    @pl.when(jnp.logical_not(slow))
    def _():
        for bin_at in others:
            for core in (0, 1):
                greet(2 * m + core, bin_at)
        greet(2 * m + 1 - p, k)

    loads = [
        pltpu.make_async_copy(density, dense, load_sem.at[0]),
        pltpu.make_async_copy(velocity, speed, load_sem.at[1]),
        pltpu.make_async_copy(growth, cells_f.at[0], load_sem.at[2]),
        pltpu.make_async_copy(rate, cells_f.at[1], load_sem.at[3]),
        pltpu.make_async_copy(direction, cells_i.at[0], load_sem.at[4]),
        pltpu.make_async_copy(neighbour, cells_i.at[1], load_sem.at[5]),
        pltpu.make_async_copy(yields, yield_row, load_sem.at[6]),
    ]
    for load in loads:
        load.start()

    @pl.when(slow)
    def _():
        pl.semaphore_wait(barrier, 2 * group - 1)
        for i in range(1, group + group // 2):
            pl.semaphore_signal(
                call_sem, inc=1, device_id=(i // group, i % group), device_id_type=MESH
            )

    for load in loads:
        load.wait()

    for q in range(rows):
        sent_rows[q] = dense[pl.ds(q, local_bins, stride=rows), :]
    sent_cells[0:1] = speed[0]
    sent_cells[1:2] = speed[1]
    sent_cells[2:3] = cells_f[0, pl.ds(k, 1), :]
    sent_cells[3:4] = cells_f[1, pl.ds(k, 1), :]
    sent_cells[4:5] = cells_i[0, pl.ds(k, 1), :].astype(jnp.float32)
    sent_cells[5:6] = cells_i[1, pl.ds(k, 1), :].astype(jnp.float32)
    sent_cells[6:8] = jnp.zeros((2, sent_cells.shape[1]), jnp.float32)

    @pl.when(jnp.logical_not(slow))
    def _():
        pl.semaphore_wait(
            barrier, 2 * group - 1 + jnp.where(beside, 2, 0) - jnp.where(slow_pair, 1, 0)
        )

    mine = pl.ds(pl.multiple_of(PAD + local_bins * k, PAD), local_bins)
    first_chip = p * (rows // 2)

    def target(q, layer):
        half = lax.div(q, 2)
        odd = q - 2 * half
        shift = (layer + 1) // 2
        core = odd if layer % 2 == 0 else 1 - odd
        return core, first_chip + half + shift - 2 * shift * core

    def cases(core, chip):
        near = jnp.logical_and(chip >= 0, chip < group)
        here = jnp.logical_and(chip == k, core == p)
        return jnp.logical_and(near, jnp.logical_not(here)), here

    def remote_row(q, layer, cell, bin_at):
        return pltpu.make_async_remote_copy(
            sent_rows.at[q], n0.at[STEPS - layer, mine], row_send.at[layer * rows + q],
            row_recv.at[layer], device_id=(cell, bin_at), device_id_type=MESH,
        )

    def remote_cell(layer, cell, bin_at):
        return pltpu.make_async_remote_copy(
            sent_cells, cells.at[STEPS - layer], cell_send.at[layer], cell_recv.at[layer],
            device_id=(cell, bin_at), device_id_type=MESH,
        )

    far_cell = jnp.where(p == 0, c - 1, c + 1)
    far_first = jnp.where(p == 0, group, -group)
    far = []
    for u, layer in ((0, 1), (1, 2), (2, 3), (0, 3)):
        far.append((jnp.where(p == 0, u, rows - 1 - u), layer))

    def send_far():
        for q, layer in far:
            _, chip = target(q, layer)
            remote_row(q, layer, far_cell, chip + far_first).start()

    @pl.when(jnp.logical_and(beside, p == 1))
    def _():
        send_far()

    called_0 = jnp.logical_and(called, p == 0)

    def send_rows(layer):
        for chip in others:
            for core in (0, 1):
                q = 2 * (chip - first_chip) + (1 + layer if core else -layer)
                go = jnp.logical_and(q >= 0, q < rows)
                if core == 0:
                    early = jnp.logical_and(layer == 0, chip == 0)
                    go = jnp.logical_and(go, jnp.logical_not(jnp.logical_and(called_0, early)))

                @pl.when(go)
                def _():
                    remote_row(q, layer, 2 * m + core, chip).start()

        for core in (0, 1):
            q = 2 * (k - first_chip) + (1 + layer if core else -layer)
            go = jnp.logical_and(q >= 0, q < rows)

            @pl.when(jnp.logical_and(go, p != core))
            def _():
                remote_row(q, layer, 2 * m + core, k).start()

            @pl.when(jnp.logical_and(go, p == core))
            def _():
                pltpu.make_async_copy(
                    sent_rows.at[q], n0.at[STEPS - layer, mine], row_recv.at[layer]
                ).start()

    send_rows(0)

    @pl.when(jnp.logical_and(beside, p == 0))
    def _():
        send_far()

    for layer in range(STEPS):
        core, chip = target(k, layer)
        go, here = cases(core, chip)
        outside = jnp.logical_or(chip < 0, chip >= group)

        @pl.when(go)
        def _():
            remote_cell(layer, 2 * m + core, chip).start()

        @pl.when(here)
        def _():
            pltpu.make_async_copy(
                sent_cells, cells.at[STEPS - layer], cell_recv.at[layer]
            ).start()

        @pl.when(jnp.logical_and(outside, beside))
        def _():
            remote_cell(layer, far_cell, chip + far_first).start()

    @pl.loop(1, STEPS + 1)
    def _(layer):
        send_rows(layer)

    spread = jnp.broadcast_to(yield_row[...], (bins, bins))
    spread = pltpu.roll(spread, 0, 1, stride=1, stride_axis=0)
    at_b = lax.broadcasted_iota(jnp.int32, (bins, bins), 0)
    at_a = lax.broadcasted_iota(jnp.int32, (bins, bins), 1)
    high, low = split(jnp.where(at_a >= at_b, spread, 0.0))
    table[...] = high
    table_low[...] = low

    lane = n0.shape[-1]
    zero = jnp.zeros((PAD, lane), jnp.float32)
    for buffer in (n0, n1, n2, n3):
        for place in range(buffer.shape[0]):
            buffer[place, 0:PAD] = zero

    body = pl.ds(PAD, bins)
    mate_id = (2 * m + 1 - p, k)
    first = 2 * (m * group + k)
    last = 2 * pairs * rows - 1

    def row_at(place):
        return first + jnp.where(p == 0, place - STEPS, STEPS + 1 - place)

    def is_row(layer):
        row = row_at(STEPS - layer)
        return jnp.logical_and(row >= 0, row <= last)

    for layer in range(1, STEPS + 1):
        @pl.when(jnp.logical_not(is_row(layer)))
        def _():
            n0[STEPS - layer, PAD:] = jnp.zeros((bins, lane), jnp.float32)
            if layer < STEPS:
                cells[STEPS - layer] = jnp.zeros(cells.shape[1:], jnp.float32)

    @pl.when(called)
    def _():
        pl.semaphore_wait(call_sem, 1)

        @pl.when(p == 0)
        def _():
            remote_row(0, 0, 0, 0).start()

    def arrived(layer):
        @pl.when(is_row(layer))
        def _():
            there = n0.at[STEPS - layer, body]
            pltpu.make_async_copy(there, there, row_recv.at[layer]).wait()

    def cell_arrived(layer):
        @pl.when(is_row(layer))
        def _():
            there = cells.at[STEPS - layer]
            pltpu.make_async_copy(there, there, cell_recv.at[layer]).wait()

    def to_mate(layer):
        return pltpu.make_async_remote_copy(
            n0.at[STEPS - layer, body], n0.at[STEPS + 1 + layer, body],
            mate_send.at[layer], mate_recv.at[layer], device_id=mate_id, device_id_type=MESH,
        )

    def cell_to_mate(layer):
        return pltpu.make_async_remote_copy(
            cells.at[STEPS - layer], cells.at[STEPS + 1 + layer],
            mate_cell_send.at[layer], mate_cell_recv.at[layer],
            device_id=mate_id, device_id_type=MESH,
        )

    gifts = [to_mate(layer) for layer in range(STEPS)]
    cell_gifts = [cell_to_mate(layer) for layer in range(STEPS - 1)]
    offset = lax.broadcasted_iota(jnp.int32, (CHUNK, lane), 0).astype(jnp.float32)
    first_size = 0.5 + 0.5 * (offset + 0.5) / bins

    def weigh(place):
        row = row_at(place)
        mine_0, mine_1 = cells[place, 0:1], cells[place, 1:2]
        down = cells[place, 4:5] == 0.0
        below = jnp.where(down, mine_0, 0.0) * jnp.where(row > 0, 1.0, 0.0)
        above = jnp.where(down, 0.0, mine_0) * jnp.where(row < last, 1.0, 0.0)
        core = jnp.where(p == 0, 1.0, 0.0)
        return (
            mine_0 + mine_1, mine_1, core * below + (1.0 - core) * above,
            core * above + (1.0 - core) * below, cells[place, 2:3], cells[place, 3:4],
            jnp.broadcast_to(cells[place, 5:6].astype(jnp.int32), (CHUNK, lane)),
        )

    def births(source, at):
        high, low = split(source[at, PAD:])
        both = jnp.dot(
            table[...], jnp.concatenate([high, low], axis=1), preferred_element_type=jnp.float32
        )
        rest = jnp.dot(table_low[...], high, preferred_element_type=jnp.float32)
        return both[:, :lane] + both[:, lane:] + rest

    def advance(source, goal, at, weights, birth, with_before=True, with_after=True):
        total, side, before, after, grow, fragment, lookup = weights
        for i in range(bins // CHUNK):
            low, high = i * CHUNK, (i + 1) * CHUNK
            n = source[at, PAD + low : PAD + high]
            lower = source[at, PAD - 1 + low : PAD - 1 + high]
            lateral = jnp.take_along_axis(n, lookup, axis=1, mode="promise_in_bounds")
            size = first_size + 0.5 * low / bins
            moved = total * n - side * lateral
            if with_before:
                moved -= before * source[at - 1, PAD + low : PAD + high]
            if with_after:
                moved -= after * source[at + 1, PAD + low : PAD + high]
            goal[at - 1, PAD + low : PAD + high] = (
                n - size * moved - grow * (n - lower) + fragment * birth[low:high]
            )

    arrived(0)
    gifts[0].start()
    for layer in range(STEPS):
        cell_arrived(layer)
        if layer < STEPS - 1:
            cell_gifts[layer].start()
    arrived(1)
    gifts[1].start()
    weights = {place: weigh(place) for place in (3, 2, 1)}
    birth_3, birth_2 = births(n0, 3), births(n0, 2)
    gifts[0].wait_recv()
    advance(n0, n1, 3, weights[3], birth_3)
    birth_4 = births(n0, 4)
    arrived(2)
    gifts[2].start()
    advance(n0, n1, 2, weights[2], birth_2)
    advance(n0, n1, 1, weights[1], births(n0, 1), with_before=False)
    for gift in cell_gifts:
        gift.wait_recv()
    weights.update({place: weigh(place) for place in (4, 5)})
    gifts[1].wait_recv()
    advance(n0, n1, 4, weights[4], birth_4)
    advance(n0, n1, 5, weights[5], births(n0, 5), with_after=False)
    advance(n1, n2, 2, weights[3], births(n1, 2))
    advance(n1, n2, 1, weights[2], births(n1, 1), with_before=False)
    advance(n1, n2, 3, weights[4], births(n1, 3), with_after=False)
    advance(n2, n3, 1, weights[3], births(n2, 1), with_before=False, with_after=False)

    arrived(3)
    gifts[2].wait_recv()
    for i in range(bins // CHUNK):
        low, high = i * CHUNK, (i + 1) * CHUNK
        here = pl.ds(PAD + low, CHUNK)
        size = first_size + 0.5 * low / bins
        one = n1[0, here] + size * (weights[1][2] * n0[0, here])
        two = n2[0, here] + size * (weights[2][2] * one)
        other_one = n1[4, here] + size * (weights[5][3] * n0[6, here])
        other_two = n2[2, here] + size * (weights[4][3] * other_one)
        n3[0, here] += size * (weights[3][2] * two + weights[3][3] * other_two)

    slot = 2 * k + p
    upper = slot >= rows
    holder = 2 * m + jnp.where(upper, 1, 0)
    slot = jnp.where(upper, slot - rows, slot)
    holds = holder == c

    def part(j):
        return n3.at[0, pl.ds(pl.multiple_of(PAD + local_bins * j, PAD), local_bins)]

    def remote_back(j):
        return pltpu.make_async_remote_copy(
            part(j), back.at[slot], back_send.at[j], back_recv,
            device_id=(holder, j), device_id_type=MESH,
        )

    @pl.when(holds)
    def _():
        pltpu.make_async_copy(part(k), back.at[slot], back_recv).start()

    for j in (0, 1):
        @pl.when(jnp.logical_not(jnp.logical_and(holds, k == j)))
        def _():
            remote_back(j).start()

    for j in others:
        @pl.when(j > 1)
        def _():
            remote_back(j).start()

    @pl.when(jnp.logical_and(k > 1, jnp.logical_not(holds)))
    def _():
        remote_back(k).start()

    for gift in gifts + cell_gifts:
        gift.wait_send()

    @pl.when(beside)
    def _():
        for q, layer in far:
            remote_row(q, layer, far_cell, k).wait_send()

    for layer in range(STEPS + 1):
        if layer < STEPS:
            core, chip = target(k, layer)
            go, _ = cases(core, chip)
            outside = jnp.logical_or(chip < 0, chip >= group)

            @pl.when(jnp.logical_or(go, jnp.logical_and(outside, beside)))
            def _():
                remote_cell(layer, far_cell, k).wait_send()

        @pl.loop(0, rows)
        def _(q):
            core, chip = target(q, layer)
            go, _ = cases(core, chip)

            @pl.when(go)
            def _():
                remote_row(q, layer, far_cell, k).wait_send()

    pltpu.make_async_copy(back, back, back_recv).wait()
    for q in range(rows):
        out[pl.ds(q, local_bins, stride=rows), :] = back[q]

    for j in others:
        remote_back(j).wait_send()

    @pl.when(jnp.logical_not(holds))
    def _():
        remote_back(k).wait_send()


def on_device(pairs, group, density, velocity, growth, rate, yields, direction, neighbour):
    local_bins, rows, lane = density.shape
    bins = yields.shape[0]
    f32, dma = jnp.float32, pltpu.SemaphoreType.DMA
    padded = PAD + bins
    result = pl.pallas_call(
        functools.partial(kernel, pairs, group, rows, local_bins, bins),
        out_shape=pltpu.VMEM((local_bins * rows, lane), f32),
        in_specs=[pl.BlockSpec(memory_space=pltpu.HBM)] * 7,
        out_specs=pl.BlockSpec(memory_space=pltpu.VMEM),
        scratch_shapes=[
            pltpu.VMEM((local_bins * rows, lane), f32),
            pltpu.VMEM((2, 1, lane), f32),
            pltpu.VMEM((2, rows, lane), f32),
            pltpu.VMEM((2, rows, lane), jnp.int32),
            pltpu.VMEM((1, bins), f32),
            pltpu.VMEM((rows, local_bins, lane), f32),
            pltpu.VMEM((8, lane), f32),
            pltpu.VMEM((rows, local_bins, lane), f32),
            pltpu.VMEM((2 * STEPS + 1, padded, lane), f32),
            pltpu.VMEM((2 * STEPS - 1, padded, lane), f32),
            pltpu.VMEM((2 * STEPS - 3, padded, lane), f32),
            pltpu.VMEM((1, padded, lane), f32),
            pltpu.VMEM((2 * STEPS, 8, lane), f32),
            pltpu.VMEM((bins, bins), jnp.bfloat16),
            pltpu.VMEM((bins, bins), jnp.bfloat16),
            dma((7,)),
            dma((STEPS,)),
            dma((STEPS,)),
            dma((4 * rows,)),
            dma((STEPS + 1,)),
            dma((STEPS,)),
            dma((STEPS,)),
            dma((group,)),
            dma,
            dma((STEPS - 1,)),
            dma((STEPS - 1,)),
            pltpu.SemaphoreType.REGULAR,
        ],
        compiler_params=pltpu.CompilerParams(
            collective_id=0, has_side_effects=True, vmem_limit_bytes=60 * 2**20
        ),
        cost_estimate=pl.CostEstimate(flops=10**9, bytes_accessed=2**21, transcendentals=0),
    )(
        density.reshape(local_bins * rows, lane), velocity, growth, rate, yields.reshape(1, bins),
        direction, neighbour,
    )
    return result.reshape(density.shape)


def solution(mesh):
    return jax.shard_map(
        functools.partial(on_device, mesh.shape["cell"] // 2, mesh.shape["bin"]),
        mesh=mesh,
        in_specs=(
            P("bin", "cell", None),
            P(None, ("cell", "bin"), None),
            P("cell", None),
            P("cell", None),
            P(),
            P("cell", None),
            P("cell", None),
        ),
        out_specs=P("bin", "cell", None),
        check_vma=False,
    )
```
